128 devices in a mesh: tm: 16 (over y, x_lo, core), space: 8 (over x_hi, z).
Axes of the slice: x: 4 (x_hi: 2, x_lo: 2; x = x_hi * 2 + x_lo), y: 4, z: 4, core: 2. Of those that a mesh axis runs over, the one named last changes fastest.
Arguments:
- snapshots: bfloat16 [16384, 65536], P('space', 'tm'), may hold values from -60 to 60
- basis: bfloat16 [16384, 64], P('space'), may hold values from -0.046875 to 0.046875
Outputs:
- reduced_rates: float32 [64, 65536], P(None, ('tm', 'space'))
- gram_quad: float32 [2080, 2080], P('tm', 'space')
- gram_side: float32 [65, 2145], replicated
- rhs: float32 [2145, 64], replicated
The draws below stay inside these ranges and needn't reach their ends.
All inputs are finite; a program needn't handle non-finite values.
Results may differ from the reference program's by a relative error of at most 0.0003.
Values sent between devices are 32-bit elements; how exact they have to be, the bound alone decides.
A program may use at most 128 MiB of HBM per device.

```python
import jax
import jax.numpy as jnp
import numpy as np
from jax import lax

R = 64
DOF = 16384
TIME = 65536


def draw_snapshots(key, part):
    keys = jax.random.split(jax.random.fold_in(key, 7), 5)
    noise = jnp.clip(jax.random.normal(keys[0], (DOF, TIME), jnp.float32), -5.0, 5.0)
    row_scale = jnp.exp(jax.random.uniform(keys[1], (DOF, 1), jnp.float32) * 2.302585)
    col_scale = jnp.exp(jax.random.uniform(keys[2], (1, TIME), jnp.float32) * 2.302585)
    field = jnp.clip(jax.random.normal(keys[3], (DOF, 1), jnp.float32), -5.0, 5.0)
    weight = jax.random.uniform(keys[4], (1, TIME), jnp.float32, -1.0, 1.0)
    values = (noise * row_scale * col_scale + 2.0 * field * weight * col_scale) * 0.1
    return jnp.clip(values, -60.0, 60.0).astype(jnp.bfloat16)


def block_levels(stream_key, extent, pieces, low, largest):
    def one(axis_at, shards_of):
        heights = jax.random.uniform(jax.random.fold_in(jax.random.fold_in(stream_key, 6), axis_at), (shards_of,), jnp.float32, low / len(pieces), largest / len(pieces))
        return jnp.repeat(jnp.exp(heights), extent[axis_at] // shards_of).reshape((-1,) + (1,) * (len(extent) - axis_at - 1))

    level = one(*pieces[0])
    for cut in pieces[1:]:
        level = level * one(*cut)
    return level


def gaussian(rng, shape, scale, most, pieces=(), held_as=jnp.bfloat16):
    result = jax.random.normal(rng, shape, jnp.float32) * scale
    if len(pieces) > 0:
        result = block_levels(rng, shape, pieces, -0.22, 0.18) * result
    return jnp.clip(result, min=-most, max=most).astype(held_as)


def setup_inputs(seed: int = 0) -> dict:
    streams_of = jax.random.split(jax.random.key(seed), 3)
    snapshots = draw_snapshots(jax.random.fold_in(streams_of[2], 71), 0)
    basis = gaussian(streams_of[1], (DOF, R), DOF ** -0.5, 0.046875, ((0, 8),))
    return dict(snapshots=snapshots, basis=basis)


def reference(snapshots, basis):
    reduced = lax.dot_general(basis, snapshots, (((0,), (0,)), ((), ())), preferred_element_type=jnp.float32)
    ghost_left = 2.0 * reduced[:, :1] - reduced[:, 1:2]
    ghost_right = 2.0 * reduced[:, -1:] - reduced[:, -2:-1]
    extended = jnp.concatenate([ghost_left, reduced, ghost_right], axis=1)
    rates = 0.5 * (extended[:, 2:] - extended[:, :-2])
    upper_i, upper_j = np.triu_indices(R)
    quad = reduced[upper_i] * reduced[upper_j]
    side = jnp.concatenate([jnp.ones((1, reduced.shape[1]), jnp.float32), reduced], axis=0)
    feats = jnp.concatenate([quad, side], axis=0)
    scale = 1.0 / TIME
    dims = (((1,), (1,)), ((), ()))
    high = lax.Precision.HIGHEST
    gram_quad = lax.dot_general(quad, quad, dims, precision=high) * scale
    gram_side = lax.dot_general(side, feats, dims, precision=high) * scale
    rhs = lax.dot_general(feats, rates, dims, precision=high) * scale
    return rates, gram_quad, gram_side, rhs
```

```python
import functools

import jax
import jax.numpy as jnp
import numpy as np
from jax import lax
from jax.experimental import pallas as pl
from jax.experimental.pallas import tpu as pltpu
from jax.sharding import PartitionSpec as P

F32 = jnp.float32
BF16 = jnp.bfloat16
MESH = pl.DeviceIdType.MESH
ROWS_BY_ROWS = (((1,), (1,)), ((), ()))

MODES = 64
SPACE = 8
TIMES = 16
BLOCK = 512
SLAB = SPACE * BLOCK
MINE = 272
SENT = 264


def pair_of(k):
    i = 0
    while k >= MODES - i:
        k -= MODES - i
        i += 1
    return i, i + k


def half_plan(row):
    block, inside = divmod(row, 128)
    runs = []
    for r in range(8):
        i, j = pair_of(130 * block + inside + r)
        if not runs or runs[-1][1] != i:
            at = j - r + 8
            runs.append((r, i, at % 8, at - at % 8))
    return runs


def build_plan():
    segments = []
    for row in range(0, 2048, 16):
        low, high = half_plan(row), half_plan(row + 8)
        pure = len(low) == 1 and len(high) == 1 and low[0][1:3] == high[0][1:3]
        if not pure:
            segments.append((row, 16, (low, high)))
            continue
        run = low[0]
        last = segments[-1] if segments else None
        if (
            last
            and not isinstance(last[2], tuple)
            and last[2][0] == list(run)[1]
            and last[2][1] == run[2]
            and last[2][2] + last[1] == run[3]
        ):
            segments[-1] = (last[0], last[1] + 16, last[2])
        else:
            segments.append((row, 16, [run[1], run[2], run[3]]))
    return segments


def kernel(
    snap, basis, rates_o, gram_o, lo_o,
    AH, AL, MH, ML, LH, LL, BT, XA, XS, LQ, sbuf, rbuf, accs, crecv, isend, irecv,
    accl, turn, lom, lor, los, LOA,
    snap_sem, rs_s, rs_r, ag_s, ag_r, halo_s, halo_r, core_s, core_r, ici_s, ici_r,
    lo_s, lo_r, lt_s, lt_r, lx_s, lx_r, lc_s, lc_r,
):
    a = lax.axis_index("tm")
    s = lax.axis_index("space")
    y, xl, c = a // 4, (a // 2) % 2, a % 2
    xh, z = s // 4, s % 4

    def space_to(o):
        return ((xh + o // 4) % 2) * 4 + (z + o % 4) % 4

    def space_from(o):
        return ((xh + 2 - o // 4) % 2) * 4 + (z + 4 - o % 4) % 4

    def chip_to(o):
        return ((y + o // 2) % 4) * 2 + (xl + o % 2) % 2

    def copy(src, dst, ss, rs, tm, sp):
        return pltpu.make_async_remote_copy(
            src_ref=src, dst_ref=dst, send_sem=ss, recv_sem=rs, device_id=(tm, sp), device_id_type=MESH
        )

    def loop(low, high, step):
        def inner(k, carry):
            step(k)
            return carry

        lax.fori_loop(low, high, inner, 0)

    barrier = pltpu.get_barrier_semaphore()
    loop(1, 8, lambda o: pl.semaphore_signal(barrier, inc=1, device_id=(a, space_to(o)), device_id_type=MESH))
    loop(1, 16, lambda o: pl.semaphore_signal(barrier, inc=1, device_id=((a + o) % 16, s), device_id_type=MESH))

    def fetch(k):
        cols = pl.ds(pl.multiple_of(BLOCK * space_to(7 - k), BLOCK), BLOCK)
        into = pl.ds(pl.multiple_of(BLOCK * k, BLOCK), BLOCK)
        return pltpu.make_async_copy(snap.at[:, cols], AH.at[:, into], snap_sem.at[k])

    loop(0, 8, lambda k: fetch(k).start())
    BT[...] = basis[...].astype(F32).T.astype(BF16)

    def project(k):
        fetch(k).wait()
        into = pl.ds(pl.multiple_of(BLOCK * k, BLOCK), BLOCK)
        sbuf[k] = jnp.dot(BT[...], AH[:, into], preferred_element_type=F32)

    def share(k):
        o = 7 - k
        return copy(sbuf.at[k], rbuf.at[o - 1], rs_s.at[o - 1], rs_r.at[o - 1], a, space_to(o))

    project(0)
    pl.semaphore_wait(barrier, 22)
    share(0).start()

    def middle(k):
        project(k)
        share(k).start()

    loop(1, 7, middle)
    project(7)

    def add_share(o):
        share(7 - o).wait_recv()
        sbuf[7] += rbuf[o - 1]

    loop(1, 8, add_share)
    XA[s + 1] = sbuf[7]

    def spread(o):
        mine = XA.at[s + 1]
        return copy(mine, mine, ag_s.at[o - 1], ag_r.at[o - 1], a, space_to(o))

    def arrival(o):
        theirs = XA.at[space_from(o) + 1]
        return copy(theirs, theirs, ag_s.at[o - 1], ag_r.at[o - 1], a, space_to(o))

    loop(1, 8, lambda o: spread(o).start())

    segments = build_plan()

    def split(value):
        high = value.astype(BF16)
        return high, (value - high.astype(F32)).astype(BF16)

    LQ[...] = jnp.where(lax.broadcasted_iota(jnp.int32, (64, BLOCK), 0) % 8 == 4, 1.0, 0.0).astype(F32)
    LH[192:256, :] = jnp.zeros((64, SLAB), BF16)
    LL[192:256, :] = jnp.zeros((64, SLAB), BF16)
    row8 = lax.broadcasted_iota(jnp.int32, (8, BLOCK), 0)

    def build(o):
        @pl.when(o > 0)
        def _():
            arrival(o).wait_recv()

        b = space_from(o)
        cols = pl.ds(pl.multiple_of(BLOCK * b, BLOCK), BLOCK)
        x = XA[b + 1]
        pad = jnp.zeros((8, BLOCK), F32)
        xp = jnp.concatenate([pad, x, pad], axis=0)
        XS[0] = xp
        for shift in range(1, 8):
            XS[shift] = pltpu.roll(xp, 80 - shift, 0)

        def row(i):
            return XA[b + 1, i : i + 1, :]

        def half(runs):
            value = None
            for first, i, shift, base in runs:
                term = row(i) * XS[shift, base : base + 8, :]
                value = term if value is None else jnp.where(row8 >= first, term, value)
            return value

        for first, count, what in segments:
            if isinstance(what, tuple):
                value = jnp.concatenate([half(what[0]), half(what[1])], axis=0)
            else:
                i, shift, base = what
                value = row(i) * XS[shift, base : base + count, :]
            high, low = split(value)
            AH[first : first + count, cols] = high
            AL[first : first + count, cols] = low
        for n in range(8):
            for q, k in enumerate((260 * n + 128, 260 * n + 129, 260 * n + 258, 260 * n + 259)):
                i, j = pair_of(k)
                LQ[8 * n + q : 8 * n + q + 1, :] = row(i) * row(j)
        high, low = split(x)
        LH[0:64, cols] = high
        LL[0:64, cols] = low
        high, low = split(LQ[...])
        LH[128:192, cols] = high
        LL[128:192, cols] = low
        at = pl.multiple_of(8 * s, 8)
        high, low = split(jnp.concatenate([LQ[pl.ds(at, 8), :], XA[b + 1, pl.ds(at, 8), :]], axis=0))
        MH[256:272, cols] = high
        ML[256:272, cols] = low

    loop(0, 8, build)

    up, down = (a + 1) % 16, (a + 15) % 16
    halo = (
        copy(XA.at[8, :, 384:512], XA.at[0, :, 384:512], halo_s.at[0], halo_r.at[0], up, s),
        copy(XA.at[1, :, 0:128], XA.at[9, :, 0:128], halo_s.at[1], halo_r.at[1], down, s),
    )
    halo[0].start()
    halo[1].start()
    own = pl.ds(pl.multiple_of(256 * s, 256), 256)
    MH[0:256, :] = AH[own, :]
    ML[0:256, :] = AL[own, :]
    halo[0].wait()
    halo[1].wait()
    tail = XA[0, :, 384:512]
    ghost = 2.0 * XA[1, :, 0:1] - XA[1, :, 1:2]
    XA[0, :, 384:512] = jnp.where(a == 0, jnp.broadcast_to(ghost, (64, 128)), tail)
    head = XA[9, :, 0:128]
    ghost = 2.0 * XA[8, :, 511:512] - XA[8, :, 510:511]
    XA[9, :, 0:128] = jnp.where(a == 15, jnp.broadcast_to(ghost, (64, 128)), head)
    lane = lax.broadcasted_iota(jnp.int32, (64, BLOCK), 1)

    def rates_of(b):
        x = XA[b + 1]
        before = jnp.where(lane == 0, jnp.broadcast_to(XA[b, :, 511:512], x.shape), pltpu.roll(x, 1, 1))
        after = jnp.where(lane == BLOCK - 1, jnp.broadcast_to(XA[b + 2, :, 0:1], x.shape), pltpu.roll(x, BLOCK - 1, 1))
        return 0.5 * (after - before)

    def rate_rows(b):
        cols = pl.ds(pl.multiple_of(BLOCK * b, BLOCK), BLOCK)
        high, low = split(rates_of(b))
        LH[64:128, cols] = high
        LL[64:128, cols] = low

    loop(0, 8, rate_rows)
    rates_o[...] = rates_of(s)

    def products(high, low):
        out = lax.dot_general(MH[...], high, ROWS_BY_ROWS, preferred_element_type=F32)
        out += lax.dot_general(ML[...], high, ROWS_BY_ROWS, preferred_element_type=F32)
        return out + lax.dot_general(MH[...], low, ROWS_BY_ROWS, preferred_element_type=F32)

    accl[...] = products(LH[...], LL[...])
    turn[0:272, :] = accl[:, 128:256]
    turn[272:384, :] = jnp.zeros((112, 128), F32)
    for k in range(3):
        turned = turn[128 * k : 128 * k + 128, :].T
        for t in range(16):
            lom[t, 32 + 8 * k : 40 + 8 * k, :] = turned[8 * (t // 2) : 8 * (t // 2) + 8, :]
    for t in range(16):
        lom[t, 0:16, :] = accl[16 * t : 16 * t + 16, 0:128]
        lom[t, 16:32, :] = accl[256:272, 0:128]

    def lo_share(o):
        to = (a + o) % 16
        return copy(lom.at[to], lor.at[o], lo_s.at[o - 1], lo_r.at[o - 1], to, s)

    def lo_times(o):
        part = LOA.at[0, a]
        return copy(part, part, lt_s.at[o - 1], lt_r.at[o - 1], (a + o) % 16, s)

    def lo_times_arrival(o):
        part = LOA.at[0, (a + 16 - o) % 16]
        return copy(part, part, lt_s.at[o - 1], lt_r.at[o - 1], (a + o) % 16, s)

    def lo_space(o):
        part = pl.ds(9 * c, 9)
        return copy(LOA.at[0, part], LOA.at[o, part], lx_s.at[o - 1], lx_r.at[o - 1], a, space_to(o))

    def lo_core():
        part = LOA.at[1:8, pl.ds(9 * c, 9)]
        return copy(part, part, lc_s, lc_r, a + 1 - 2 * c, s)

    def lo_core_arrival():
        part = LOA.at[1:8, pl.ds(9 * (1 - c), 9)]
        return copy(part, part, lc_s, lc_r, a + 1 - 2 * c, s)

    loop(1, 16, lambda o: lo_share(o).start())

    def core_share(t):
        return copy(accs.at[t, 1 - c, 0:SENT], crecv.at[t], core_s.at[t], core_r.at[t], a + 1 - 2 * c, s)

    def chip_share(t):
        o = 7 - t
        return copy(isend.at[t], irecv.at[o - 1], ici_s.at[o - 1], ici_r.at[o - 1], chip_to(o) * 2 + c, s)

    def pass_on(t):
        core_share(t).wait_recv()
        isend[t] = accs[t, c, 0:SENT, :] + crecv[t]
        chip_share(t).start()

    def tile(t):
        rows = pl.ds(pl.multiple_of(256 * chip_to(7 - t), 256), 256)
        out = products(AH[rows, :], AL[rows, :])
        accs[t, 0] = out[:, 0:128]
        accs[t, 1] = out[:, 128:256]
        core_share(t).start()

        @pl.when(t > 0)
        def _():
            pass_on(t - 1)

        @pl.when(t == 2)
        def _():
            loop(1, 16, lambda o: lo_share(o).wait_recv())
            lor[0] = lom[a]
            los[...] = jnp.zeros((56, 128), F32)

            def add(k):
                los[...] += lor[(a + 16 - k) % 16]

            loop(0, 16, add)
            LOA[0, a] = los[0:16, :]
            LOA[0, 16] = los[16:32, :]
            LOA[0, 17] = jnp.zeros((16, 128), F32)
            for k in range(3):
                LOA[0, 17, k : k + 1, :] = los[36 + 8 * k : 37 + 8 * k, :]
            loop(1, 16, lambda o: lo_times(o).start())

        @pl.when(t == 4)
        def _():
            loop(1, 16, lambda o: lo_times_arrival(o).wait_recv())
            loop(1, 16, lambda o: lo_times(o).wait_send())
            loop(1, 8, lambda o: lo_space(o).start())

        @pl.when(t == 7)
        def _():
            loop(1, 8, lambda o: lo_space(o).wait_recv())
            lo_core().start()

    loop(0, 8, tile)

    scale = 1.0 / (SLAB * TIMES)
    core_share(7).wait_recv()
    turn[0:SENT, :] = accs[7, c, 0:SENT, :] + crecv[7]

    def add_chip(o):
        chip_share(7 - o).wait_recv()
        turn[0:SENT, :] += irecv[o - 1]

    loop(1, 8, add_chip)
    left, right, four = (turn[128 * k : 128 * k + 128, :].T for k in range(3))

    def place(left, right, four):
        low = lax.broadcasted_iota(jnp.int32, left.shape, 1) < 2
        moved = pltpu.roll(right, 2, 1)
        return left * scale, jnp.where(low, four, moved) * scale, jnp.where(low, moved, four) * scale

    first, second, third = place(left, right, four)
    gram_o[0:128, 0:128] = first
    gram_o[0:128, 128:256] = second
    gram_o[0:128, 256:260] = third[:, 0:4]
    parts = place(los[32:40, :], los[40:48, :], los[48:56, :])
    first, second, third = (jnp.where(c == 0, part[0:2, :], part[2:4, :]) for part in parts)
    gram_o[128:130, 0:128] = first
    gram_o[128:130, 128:256] = second
    gram_o[128:130, 256:260] = third[:, 0:4]

    lo_core_arrival().wait_recv()

    def give(o):
        lo_o[space_from(o)] = LOA[o] * scale

    loop(0, 8, give)

    loop(0, 7, lambda k: share(k).wait_send())
    loop(1, 8, lambda o: spread(o).wait_send())
    loop(1, 16, lambda o: lo_share(o).wait_send())
    loop(1, 8, lambda o: lo_space(o).wait_send())
    lo_core().wait_send()
    loop(0, 8, lambda t: core_share(t).wait_send())
    loop(0, 7, lambda t: chip_share(t).wait_send())


def body(snapshots, basis):
    vmem = pl.BlockSpec(memory_space=pltpu.VMEM)
    dma = pltpu.SemaphoreType.DMA
    rates, gram_quad, lo = pl.pallas_call(
        kernel,
        out_shape=(
            jax.ShapeDtypeStruct((MODES, BLOCK), F32),
            jax.ShapeDtypeStruct((130, 260), F32),
            jax.ShapeDtypeStruct((8, 18, 16, 128), F32),
        ),
        in_specs=[pl.BlockSpec(memory_space=pl.ANY), vmem],
        out_specs=(vmem, vmem, vmem),
        scratch_shapes=[
            pltpu.VMEM((2048, SLAB), BF16),
            pltpu.VMEM((2048, SLAB), BF16),
            pltpu.VMEM((MINE, SLAB), BF16),
            pltpu.VMEM((MINE, SLAB), BF16),
            pltpu.VMEM((256, SLAB), BF16),
            pltpu.VMEM((256, SLAB), BF16),
            pltpu.VMEM((MODES, 2048), BF16),
            pltpu.VMEM((10, MODES, BLOCK), F32),
            pltpu.VMEM((8, 80, BLOCK), F32),
            pltpu.VMEM((64, BLOCK), F32),
            pltpu.VMEM((8, MODES, BLOCK), F32),
            pltpu.VMEM((7, MODES, BLOCK), F32),
            pltpu.VMEM((8, 2, MINE, 128), F32),
            pltpu.VMEM((8, SENT, 128), F32),
            pltpu.VMEM((7, SENT, 128), F32),
            pltpu.VMEM((7, SENT, 128), F32),
            pltpu.VMEM((MINE, 256), F32),
            pltpu.VMEM((384, 128), F32),
            pltpu.VMEM((16, 56, 128), F32),
            pltpu.VMEM((16, 56, 128), F32),
            pltpu.VMEM((56, 128), F32),
            pltpu.VMEM((8, 18, 16, 128), F32),
            dma((8,)), dma((7,)), dma((7,)), dma((7,)), dma((7,)), dma((2,)), dma((2,)),
            dma((8,)), dma((8,)), dma((7,)), dma((7,)),
            dma((15,)), dma((15,)), dma((15,)), dma((15,)), dma((7,)), dma((7,)), dma(()), dma(()),
        ],
        compiler_params=pltpu.CompilerParams(
            collective_id=0, has_side_effects=True, vmem_limit_bytes=60 << 20
        ),
    )(snapshots, basis)
    rows = lo[:, :16].reshape(8, 256, 128)
    extra = lo[:, 16]
    ones = lo[:, 17]
    quad = jnp.concatenate([rows[:, :128], extra[:, 0:2], rows[:, 128:], extra[:, 2:4]], axis=1)
    feats = jnp.concatenate([quad.reshape(2080, 128), extra[0, 4:5], extra[:, 8:16].reshape(64, 128)], axis=0)
    rhs = feats[:, 64:128]
    ones_quad = jnp.concatenate([ones[:, 0], ones[:, 2, 0:2], ones[:, 1], ones[:, 2, 2:4]], axis=1).reshape(1, 2080)
    ones_row = jnp.concatenate([ones_quad, jnp.ones((1, 1), F32), extra[0, 4:5, 0:64]], axis=1)
    side = jnp.concatenate([ones_row, feats[:, 0:64].T], axis=0)
    return rates, gram_quad, side, rhs


def solution(mesh):
    in_specs = (P("space", "tm"), P("space", None))
    out_specs = (P(None, ("tm", "space")), P("tm", "space"), P(), P())
    return jax.shard_map(body, mesh=mesh, in_specs=in_specs, out_specs=out_specs, check_vma=False)
```

```python
import functools

import jax
import jax.numpy as jnp
import numpy as np
from jax import lax
from jax.experimental import pallas as pl
from jax.experimental.pallas import tpu as pltpu
from jax.sharding import PartitionSpec as P

F32 = jnp.float32
BF16 = jnp.bfloat16
MESH = pl.DeviceIdType.MESH
ROWS_BY_ROWS = (((1,), (1,)), ((), ()))

MODES = 64
SPACE = 8
TIMES = 16
BLOCK = 512
HALF = 256
SLAB = SPACE * BLOCK
MINE = 272
SENT = 264


def pair_of(k):
    i = 0
    while k >= MODES - i:
        k -= MODES - i
        i += 1
    return i, i + k


def half_plan(row):
    block, inside = divmod(row, 128)
    runs = []
    for r in range(8):
        i, j = pair_of(130 * block + inside + r)
        if not runs or runs[-1][1] != i:
            at = j - r + 8
            runs.append((r, i, at % 8, at - at % 8))
    return runs


def build_plan():
    segments = []
    for row in range(0, 2048, 16):
        low, high = half_plan(row), half_plan(row + 8)
        pure = len(low) == 1 and len(high) == 1 and low[0][1:3] == high[0][1:3]
        if not pure:
            segments.append((row, 16, (low, high)))
            continue
        run = low[0]
        last = segments[-1] if segments else None
        if (
            last
            and not isinstance(last[2], tuple)
            and last[2][0] == list(run)[1]
            and last[2][1] == run[2]
            and last[2][2] + last[1] == run[3]
        ):
            segments[-1] = (last[0], last[1] + 16, last[2])
        else:
            segments.append((row, 16, [run[1], run[2], run[3]]))
    return segments


def kernel(
    snap, basis, rates_o, gram_o, side_o, rhs_o,
    AH, AL, MH, ML, LH, LL, XA, XS, LQ, sbuf, rbuf, accs, crecv, yrecv, xsend, xrecv,
    accl, turn, lom, lomr, lor, los, LOT, LOA, GS,
    snap_sem, rs_s, rs_r, ag_s, ag_r, halo_s, halo_r, core_s, core_r, y_s, y_r, x_s, x_r,
    lo_s, lo_r, lt_s, lt_r, lx_s, lx_r, lc_s, lc_r,
):
    a = lax.axis_index("tm")
    s = lax.axis_index("space")
    y, xl, c = a // 4, (a // 2) % 2, a % 2
    chip = a // 2
    sibling = a + 1 - 2 * c
    xh, z = s // 4, s % 4

    def space_to(o):
        return ((xh + o // 4) % 2) * 4 + (z + o % 4) % 4

    def space_from(o):
        return ((xh + 2 - o // 4) % 2) * 4 + (z + 4 - o % 4) % 4

    def copy(src, dst, ss, rs, tm, sp):
        return pltpu.make_async_remote_copy(
            src_ref=src, dst_ref=dst, send_sem=ss, recv_sem=rs, device_id=(tm, sp), device_id_type=MESH
        )

    def loop(low, high, step):
        def inner(k, carry):
            step(k)
            return carry

        lax.fori_loop(low, high, inner, 0)

    def half_cols(m):
        return pl.ds(pl.multiple_of(HALF * m, HALF), HALF)

    def fetch(m):
        cols = pl.ds(pl.multiple_of(BLOCK * space_to(7 - m % 8) + HALF * (m // 8), HALF), HALF)
        return pltpu.make_async_copy(snap.at[:, cols], AH.at[:, half_cols(m)], snap_sem.at[m])

    loop(0, 8, lambda m: fetch(m).start())

    barrier = pltpu.get_barrier_semaphore()

    def greet(tm, sp):
        pl.semaphore_signal(barrier, inc=1, device_id=(tm, sp), device_id_type=MESH)

    up, down = (a + 1) % 16, (a + 15) % 16
    loop(1, 8, lambda o: greet(a, space_to(o)))
    loop(1, 8, lambda o: greet(((chip + o) % 8) * 2 + c, s))
    greet(sibling, s)
    greet(up, s)
    greet(down, s)

    loop(8, 16, lambda m: fetch(m).start())

    def project(m):
        fetch(m).wait()
        sbuf[m] = jnp.dot(basis[...], AH[:, half_cols(m)], preferred_element_type=F32)

    def share(q, o):
        at = 8 * q + o
        return copy(sbuf.at[8 * q + 7 - o], rbuf.at[at], rs_s.at[at], rs_r.at[at], a, space_to(o))

    loop(0, 8, project)
    pl.semaphore_wait(barrier, 17)
    loop(0, 7, lambda m: share(0, 7 - m).start())

    def middle(m):
        project(m)

        @pl.when(m < 15)
        def _():
            share(1, 15 - m).start()

    loop(8, 16, middle)

    def spread(q, o):
        mine = XA.at[q, s + 1]
        return copy(mine, mine, ag_s.at[8 * q + o], ag_r.at[8 * q + o], a, space_to(o))

    def arrival(q, o):
        theirs = XA.at[q, space_from(o) + 1]
        return copy(theirs, theirs, ag_s.at[8 * q + o], ag_r.at[8 * q + o], a, space_to(o))

    for q in range(2):
        def add_share(o):
            share(q, o).wait_recv()
            sbuf[8 * q + 7] += rbuf[8 * q + o]

        loop(1, 8, add_share)
        XA[q, s + 1] = sbuf[8 * q + 7]
        loop(1, 8, lambda o: spread(q, o).start())

    segments = build_plan()

    def split(value):
        high = value.astype(BF16)
        return high, (value - high.astype(F32)).astype(BF16)

    LQ[...] = jnp.where(lax.broadcasted_iota(jnp.int32, (64, HALF), 0) % 8 == 4, 1.0, 0.0).astype(F32)
    LH[192:256, :] = jnp.zeros((64, SLAB), BF16)
    LL[192:256, :] = jnp.zeros((64, SLAB), BF16)
    row8 = lax.broadcasted_iota(jnp.int32, (8, HALF), 0)

    def build(q, b):
        cols = half_cols(8 * q + b)
        x = XA[q, b + 1]
        pad = jnp.zeros((8, HALF), F32)
        xp = jnp.concatenate([pad, x, pad], axis=0)
        XS[0] = xp
        for shift in range(1, 8):
            XS[shift] = pltpu.roll(xp, 80 - shift, 0)

        def row(i):
            return XA[q, b + 1, i : i + 1, :]

        def half(runs):
            value = None
            for first, i, shift, base in runs:
                term = row(i) * XS[shift, base : base + 8, :]
                value = term if value is None else jnp.where(row8 >= first, term, value)
            return value

        for first, count, what in segments:
            if isinstance(what, tuple):
                value = jnp.concatenate([half(what[0]), half(what[1])], axis=0)
            else:
                i, shift, base = what
                value = row(i) * XS[shift, base : base + count, :]
            high, low = split(value)
            AH[first : first + count, cols] = high
            AL[first : first + count, cols] = low
        for n in range(8):
            for p, k in enumerate((260 * n + 128, 260 * n + 129, 260 * n + 258, 260 * n + 259)):
                i, j = pair_of(k)
                LQ[8 * n + p : 8 * n + p + 1, :] = row(i) * row(j)
        high, low = split(x)
        LH[0:64, cols] = high
        LL[0:64, cols] = low
        high, low = split(LQ[...])
        LH[128:192, cols] = high
        LL[128:192, cols] = low
        at = pl.multiple_of(8 * s, 8)
        high, low = split(jnp.concatenate([LQ[pl.ds(at, 8), :], XA[q, b + 1, pl.ds(at, 8), :]], axis=0))
        MH[256:272, cols] = high
        ML[256:272, cols] = low

    own = pl.ds(pl.multiple_of(256 * s, 256), 256)

    def build_half(q):
        cols = pl.ds(2048 * q, 2048)
        loop(0, 8, lambda b: build(q, b))
        MH[0:256, cols] = AH[own, cols]
        ML[0:256, cols] = AL[own, cols]

    def products(high, low, cols):
        out = lax.dot_general(MH[:, cols], high, ROWS_BY_ROWS, preferred_element_type=F32)
        out += lax.dot_general(ML[:, cols], high, ROWS_BY_ROWS, preferred_element_type=F32)
        return out + lax.dot_general(MH[:, cols], low, ROWS_BY_ROWS, preferred_element_type=F32)

    def chip_at(o):
        return ((y + o % 4) % 4) * 2 + (xl + o // 4) % 2

    def tile_products(t, cols):
        rows = pl.ds(pl.multiple_of(256 * chip_at(7 - t), 256), 256)
        return products(AH[rows, cols], AL[rows, cols], cols)

    loop(1, 8, lambda o: arrival(0, o).wait_recv())
    build_half(0)

    loop(1, 8, lambda o: arrival(1, o).wait_recv())

    halo = (
        copy(XA.at[1, 8, :, 128:256], XA.at[1, 0, :, 128:256], halo_s.at[0], halo_r.at[0], up, s),
        copy(XA.at[0, 1, :, 0:128], XA.at[0, 9, :, 0:128], halo_s.at[1], halo_r.at[1], down, s),
    )
    halo[0].start()
    halo[1].start()
    build_half(1)
    halo[0].wait()
    halo[1].wait()
    tail = XA[1, 0, :, 128:256]
    ghost = 2.0 * XA[0, 1, :, 0:1] - XA[0, 1, :, 1:2]
    XA[1, 0, :, 128:256] = jnp.where(a == 0, jnp.broadcast_to(ghost, (64, 128)), tail)
    head = XA[0, 9, :, 0:128]
    ghost = 2.0 * XA[1, 8, :, HALF - 1 : HALF] - XA[1, 8, :, HALF - 2 : HALF - 1]
    XA[0, 9, :, 0:128] = jnp.where(a == 15, jnp.broadcast_to(ghost, (64, 128)), head)
    lane = lax.broadcasted_iota(jnp.int32, (64, HALF), 1)

    def rates_of(q, b):
        x = XA[q, b + 1]
        before = XA[1 - q, b + q, :, HALF - 1 : HALF]
        after = XA[1 - q, b + 1 + q, :, 0:1]
        before = jnp.where(lane == 0, jnp.broadcast_to(before, x.shape), pltpu.roll(x, 1, 1))
        after = jnp.where(lane == HALF - 1, jnp.broadcast_to(after, x.shape), pltpu.roll(x, HALF - 1, 1))
        return 0.5 * (after - before)

    for q in range(2):
        def rate_rows(b):
            high, low = split(rates_of(q, b))
            LH[64:128, half_cols(8 * q + b)] = high
            LL[64:128, half_cols(8 * q + b)] = low

        loop(0, 8, rate_rows)
        rates_o[:, HALF * q : HALF * q + HALF] = rates_of(q, s)

    accl[...] = products(LH[...], LL[...], slice(0, SLAB))
    turn[0:272, :] = accl[...]
    turn[272:384, :] = jnp.zeros((112, 256), F32)
    for k in range(3):
        lines = turn[128 * k : 128 * k + 128, 0:128].T
        for t in range(16):
            lom[t % 2, t // 2, k] = lines[8 * t : 8 * t + 8, :]
        lines = turn[128 * k : 128 * k + 128, 128:256].T
        for t in range(8):
            lom[0, t, 3 + k] = lines[8 * t : 8 * t + 8, :]
            lom[1, t, 3 + k] = lines[8 * t : 8 * t + 8, :]

    def lo_pair():
        return copy(lom.at[1 - c], lomr, lc_s.at[8], lc_r.at[8], sibling, s)

    def lo_share(o):
        to = (chip + o) % 8
        return copy(lom.at[c, to], lor.at[o], lo_s.at[o], lo_r.at[o], to * 2 + c, s)

    def lo_times(o):
        part = LOT.at[chip]
        return copy(part, part, lt_s.at[o], lt_r.at[o], ((chip + o) % 8) * 2 + c, s)

    def lo_times_arrival(o):
        part = LOT.at[(chip + 8 - o) % 8]
        return copy(part, part, lt_s.at[o], lt_r.at[o], ((chip + o) % 8) * 2 + c, s)

    def lo_space(o):
        return copy(LOA.at[0, c], LOA.at[o, c], lx_s.at[o], lx_r.at[o], a, space_to(o))

    def lo_core(o):
        return copy(LOA.at[o, c], LOA.at[o, c], lc_s.at[o], lc_r.at[o], sibling, s)

    def lo_core_arrival(o):
        return copy(LOA.at[o, 1 - c], LOA.at[o, 1 - c], lc_s.at[o], lc_r.at[o], sibling, s)

    def lo_step_1():
        lo_pair().wait()
        lom[c] += lomr[...]
        loop(1, 8, lambda o: lo_share(o).start())

    def lo_step_2():
        loop(1, 8, lambda o: lo_share(o).wait_recv())
        lor[0] = lom[c, chip]
        los[...] = jnp.zeros((6, 8, 128), F32)

        def add(k):
            los[...] += lor[(chip + 8 - k) % 8]

        loop(0, 8, add)
        LOT[chip] = los[0:3]
        loop(1, 8, lambda o: lo_times(o).start())

    lane8 = lax.broadcasted_iota(jnp.int32, (8, 128), 1)

    def lo_step_3():
        loop(1, 8, lambda o: lo_times_arrival(o).wait_recv())
        packed = LOT[0, 2]
        for k in range(8):
            LOA[0, c, k] = LOT[k, 0]
            LOA[0, c, 8 + k] = LOT[k, 1]
            if k:
                packed = jnp.where(lane8 // 16 == k, pltpu.roll(LOT[k, 2], 16 * k, 1), packed)
        LOA[0, c, 16] = packed
        LOA[0, c, 17] = jnp.zeros((8, 128), F32)
        for k in range(3):
            LOA[0, c, 17, k : k + 1, :] = los[3 + k, 4:5, :]
        lo_core(0).start()
        loop(1, 8, lambda o: lo_space(o).start())

    def forward(o):
        lo_space(o).wait_recv()
        lo_core(o).start()

    lo_pair().start()

    def core_share(t):
        return copy(accs.at[t, 1 - c, 0:SENT], crecv.at[t], core_s.at[t], core_r.at[t], sibling, s)

    def y_share(o):
        to = ((y + o % 4) % 4) * 4 + xl * 2 + c
        return copy(accs.at[7 - o, c, 0:SENT], yrecv.at[o], y_s.at[o], y_r.at[o], to, s)

    def x_share():
        return copy(xsend, xrecv, x_s, x_r, y * 4 + (1 - xl) * 2 + c, s)

    def pass_on(t):
        core_share(t).wait_recv()
        accs[t, c, 0:SENT, :] += crecv[t]

        @pl.when(t % 4 < 3)
        def _():
            y_share(7 - t).start()

    def add_y(into, low):
        into[0:SENT] = accs[7 - low, c, 0:SENT, :]

        def add(o):
            y_share(o).wait_recv()
            into[0:SENT] += yrecv[o]

        loop(low + 1, low + 4, add)

    def tile(t):
        out = tile_products(t, slice(0, SLAB))
        accs[t, 0] = out[:, 0:128]
        accs[t, 1] = out[:, 128:256]
        core_share(t).start()

        @pl.when(t > 0)
        def _():
            pass_on(t - 1)

        @pl.when(t == 0)
        def _():
            lo_step_1()

        @pl.when(t == 2)
        def _():
            lo_step_2()

        @pl.when(t == 4)
        def _():
            lo_step_3()

        @pl.when(t == 6)
        def _():
            add_y(xsend, 4)
            x_share().start()

        @pl.when(t == 7)
        def _():
            loop(1, 8, forward)

    loop(0, 8, tile)
    pass_on(7)

    scale = 1.0 / (SLAB * TIMES)
    add_y(accl.at[:, 0:128], 0)
    x_share().wait_recv()
    turn[0:SENT, 0:128] = accl[0:SENT, 0:128] + xrecv[...]
    left, right, four = (turn[128 * k : 128 * k + 128, 0:128].T for k in range(3))

    def place(left, right, four):
        low = lax.broadcasted_iota(jnp.int32, left.shape, 1) < 2
        moved = pltpu.roll(right, 2, 1)
        return left, jnp.where(low, four, moved), jnp.where(low, moved, four)

    first, second, third = place(left, right, four)
    gram_o[0:128, 0:128] = first * scale
    gram_o[0:128, 128:256] = second * scale
    gram_o[0:128, 256:260] = third[:, 0:4] * scale
    parts = place(los[3], los[4], los[5])
    first, second, third = (jnp.where(c == 0, part[0:2, :], part[2:4, :]) * scale for part in parts)
    gram_o[128:130, 0:128] = first
    gram_o[128:130, 128:256] = second
    gram_o[128:130, 256:260] = third[:, 0:4]

    loop(0, 8, lambda o: lo_core_arrival(o).wait_recv())

    wide = lax.broadcasted_iota(jnp.int32, (136, 128), 1)
    carried = jnp.zeros((136, 128), F32)
    last = jnp.zeros((136, 128), F32)
    for b in range(8):
        o = ((xh + 2 - b // 4) % 2) * 4 + (z + 4 - b % 4) % 4
        ones = LOA[o, 0, 17]
        left = jnp.concatenate([LOA[o, t % 2, t // 2] for t in range(16)] + [ones], axis=0)
        right = jnp.concatenate([LOA[o, t % 2, 8 + t // 2] for t in range(16)] + [pltpu.roll(ones, 7, 0)], axis=0)
        packed = [LOA[o, t, 16] for t in range(2)]
        four = jnp.concatenate(
            [pltpu.roll(packed[t % 2], (128 - 16 * (t // 2)) % 128, 1) if t // 2 else packed[t % 2] for t in range(16)]
            + [pltpu.roll(ones, 6, 0)],
            axis=0,
        )
        shift = 4 * b
        first, second, third = (pltpu.roll(v, shift, 1) if b else v for v in place(left, right, four))
        GS[:, 256 * b : 256 * b + 128] = jnp.where(wide < shift, carried, first)
        GS[:, 256 * b + 128 : 256 * b + 256] = jnp.where(wide < shift, first, second)
        carried = jnp.where(wide < shift, second, third)
        modes = pltpu.roll(four, 25 + 8 * b, 1)
        last = jnp.where((wide >= 33 + 8 * b) & (wide < 41 + 8 * b), modes, last)
        if b == 7:
            last = jnp.where(wide == 32, pltpu.roll(four, 28, 1), last)
    GS[:, 2048:2176] = jnp.where(wide < 32, carried, last)
    side_o[0:1, :] = GS[128:129, 0:2145] * scale
    side_o[1:65, :] = GS[0:64, 0:2145] * scale
    rhs_o[...] = GS[64:128, 0:2145] * scale

    for q in range(2):
        loop(1, 8, lambda o: share(q, o).wait_send())
        loop(1, 8, lambda o: spread(q, o).wait_send())
    loop(1, 8, lambda o: lo_share(o).wait_send())
    loop(1, 8, lambda o: lo_times(o).wait_send())
    loop(1, 8, lambda o: lo_space(o).wait_send())
    loop(0, 8, lambda o: lo_core(o).wait_send())
    loop(0, 8, lambda t: core_share(t).wait_send())
    loop(1, 4, lambda o: y_share(o).wait_send())
    loop(5, 8, lambda o: y_share(o).wait_send())
    x_share().wait_send()


def body(snapshots, basis):
    vmem = pl.BlockSpec(memory_space=pltpu.VMEM)
    dma = pltpu.SemaphoreType.DMA
    rates, gram_quad, gram_side, rhs = pl.pallas_call(
        kernel,
        out_shape=(
            jax.ShapeDtypeStruct((MODES, BLOCK), F32),
            jax.ShapeDtypeStruct((130, 260), F32),
            jax.ShapeDtypeStruct((65, 2145), F32),
            jax.ShapeDtypeStruct((64, 2145), F32),
        ),
        in_specs=[pl.BlockSpec(memory_space=pl.ANY), vmem],
        out_specs=(vmem, vmem, vmem, vmem),
        scratch_shapes=[
            pltpu.VMEM((2048, SLAB), BF16),
            pltpu.VMEM((2048, SLAB), BF16),
            pltpu.VMEM((MINE, SLAB), BF16),
            pltpu.VMEM((MINE, SLAB), BF16),
            pltpu.VMEM((256, SLAB), BF16),
            pltpu.VMEM((256, SLAB), BF16),
            pltpu.VMEM((2, 10, MODES, HALF), F32),
            pltpu.VMEM((8, 80, HALF), F32),
            pltpu.VMEM((64, HALF), F32),
            pltpu.VMEM((16, MODES, HALF), F32),
            pltpu.VMEM((16, MODES, HALF), F32),
            pltpu.VMEM((8, 2, MINE, 128), F32),
            pltpu.VMEM((8, SENT, 128), F32),
            pltpu.VMEM((8, SENT, 128), F32),
            pltpu.VMEM((SENT, 128), F32),
            pltpu.VMEM((SENT, 128), F32),
            pltpu.VMEM((MINE, 256), F32),
            pltpu.VMEM((384, 256), F32),
            pltpu.VMEM((2, 8, 6, 8, 128), F32),
            pltpu.VMEM((8, 6, 8, 128), F32),
            pltpu.VMEM((8, 6, 8, 128), F32),
            pltpu.VMEM((6, 8, 128), F32),
            pltpu.VMEM((8, 3, 8, 128), F32),
            pltpu.VMEM((8, 2, 18, 8, 128), F32),
            pltpu.VMEM((136, 2176), F32),
            dma((16,)), dma((16,)), dma((16,)), dma((16,)), dma((16,)), dma((2,)), dma((2,)),
            dma((8,)), dma((8,)), dma((8,)), dma((8,)), dma(()), dma(()),
            dma((8,)), dma((8,)), dma((8,)), dma((8,)), dma((8,)), dma((8,)), dma((9,)), dma((9,)),
        ],
        compiler_params=pltpu.CompilerParams(
            collective_id=0, has_side_effects=True, vmem_limit_bytes=60 << 20
        ),
    )(snapshots, basis.T)
    return rates, gram_quad, gram_side, rhs.T


def solution(mesh):
    in_specs = (P("space", "tm"), P("space", None))
    out_specs = (P(None, ("tm", "space")), P("tm", "space"), P(), P())
    return jax.shard_map(body, mesh=mesh, in_specs=in_specs, out_specs=out_specs, check_vma=False)
```

```python
import functools

import jax
import jax.numpy as jnp
import numpy as np
from jax import lax
from jax.experimental import pallas as pl
from jax.experimental.pallas import tpu as pltpu
from jax.sharding import PartitionSpec as P

F32 = jnp.float32
BF16 = jnp.bfloat16
MESH = pl.DeviceIdType.MESH
ROWS_BY_ROWS = (((1,), (1,)), ((), ()))

MODES = 64
SPACE = 8
TIMES = 16
BLOCK = 512
HALF = 256
SLAB = SPACE * BLOCK
MINE = 272
SENT = 264


def pair_of(k):
    i = 0
    while k >= MODES - i:
        k -= MODES - i
        i += 1
    return i, i + k


def half_plan(row):
    block, inside = divmod(row, 128)
    runs = []
    for r in range(8):
        i, j = pair_of(130 * block + inside + r)
        if not runs or runs[-1][1] != i:
            at = j - r + 8
            runs.append((r, i, at % 8, at - at % 8))
    return runs


def build_plan():
    segments = []
    for row in range(0, 2048, 16):
        low, high = half_plan(row), half_plan(row + 8)
        pure = len(low) == 1 and len(high) == 1 and low[0][1:3] == high[0][1:3]
        if not pure:
            segments.append((row, 16, (low, high)))
            continue
        run = low[0]
        last = segments[-1] if segments else None
        if (
            last
            and not isinstance(last[2], tuple)
            and last[2][0] == list(run)[1]
            and last[2][1] == run[2]
            and last[2][2] + last[1] == run[3]
        ):
            segments[-1] = (last[0], last[1] + 16, last[2])
        else:
            segments.append((row, 16, [run[1], run[2], run[3]]))
    return segments


def kernel(
    snap, basis, rates_o, gram_o, side_o, rhs_o,
    AH, AL, MH, ML, LH, LL, XA, XS, LQ, sbuf, rbuf, accs, crecv, yrecv, xsend, xrecv,
    accl, turn, lom, lomr, lor, los, LOT, LOA, GS,
    snap_sem, rs_s, rs_r, ag_s, ag_r, halo_s, halo_r, core_s, core_r, y_s, y_r, x_s, x_r,
    lo_s, lo_r, lt_s, lt_r, lx_s, lx_r, lc_s, lc_r,
):
    a = lax.axis_index("tm")
    s = lax.axis_index("space")
    y, xl, c = a // 4, (a // 2) % 2, a % 2
    chip = a // 2
    sibling = a + 1 - 2 * c
    xh, z = s // 4, s % 4

    def space_to(o):
        return ((xh + o // 4) % 2) * 4 + (z + o % 4) % 4

    def space_from(o):
        return ((xh + 2 - o // 4) % 2) * 4 + (z + 4 - o % 4) % 4

    def copy(src, dst, ss, rs, tm, sp):
        return pltpu.make_async_remote_copy(
            src_ref=src, dst_ref=dst, send_sem=ss, recv_sem=rs, device_id=(tm, sp), device_id_type=MESH
        )

    def loop(low, high, step):
        def inner(k, carry):
            step(k)
            return carry

        lax.fori_loop(low, high, inner, 0)

    def half_cols(m):
        return pl.ds(pl.multiple_of(HALF * m, HALF), HALF)

    def fetch(m):
        cols = pl.ds(pl.multiple_of(BLOCK * space_to(7 - m % 8) + HALF * (m // 8), HALF), HALF)
        return pltpu.make_async_copy(snap.at[:, cols], AH.at[:, half_cols(m)], snap_sem.at[m])

    loop(0, 8, lambda m: fetch(m).start())

    barrier = pltpu.get_barrier_semaphore()

    def greet(tm, sp):
        pl.semaphore_signal(barrier, inc=1, device_id=(tm, sp), device_id_type=MESH)

    up, down = (a + 1) % 16, (a + 15) % 16
    loop(1, 8, lambda o: greet(a, space_to(o)))
    loop(1, 8, lambda o: greet(((chip + o) % 8) * 2 + c, s))
    greet(sibling, s)
    greet(up, s)
    greet(down, s)

    loop(8, 16, lambda m: fetch(m).start())

    def project(m):
        fetch(m).wait()
        sbuf[m] = jnp.dot(basis[...], AH[:, half_cols(m)], preferred_element_type=F32)

    def share(q, o):
        at = 8 * q + o
        return copy(sbuf.at[8 * q + 7 - o], rbuf.at[at], rs_s.at[at], rs_r.at[at], a, space_to(o))

    loop(0, 8, project)
    pl.semaphore_wait(barrier, 17)
    loop(0, 7, lambda m: share(0, 7 - m).start())

    def middle(m):
        project(m)

        @pl.when(m < 15)
        def _():
            share(1, 15 - m).start()

    loop(8, 16, middle)

    def spread(q, o):
        mine = XA.at[q, s + 1]
        return copy(mine, mine, ag_s.at[8 * q + o], ag_r.at[8 * q + o], a, space_to(o))

    def arrival(q, o):
        theirs = XA.at[q, space_from(o) + 1]
        return copy(theirs, theirs, ag_s.at[8 * q + o], ag_r.at[8 * q + o], a, space_to(o))

    for q in range(2):
        def add_share(o):
            share(q, o).wait_recv()
            sbuf[8 * q + 7] += rbuf[8 * q + o]

        loop(1, 8, add_share)
        XA[q, s + 1] = sbuf[8 * q + 7]
        loop(1, 8, lambda o: spread(q, o).start())

    segments = build_plan()

    def split(value):
        high = value.astype(BF16)
        return high, (value - high.astype(F32)).astype(BF16)

    LQ[...] = jnp.where(lax.broadcasted_iota(jnp.int32, (64, HALF), 0) % 8 == 4, 1.0, 0.0).astype(F32)
    LH[192:256, :] = jnp.zeros((64, SLAB), BF16)
    LL[192:256, :] = jnp.zeros((64, SLAB), BF16)
    row8 = lax.broadcasted_iota(jnp.int32, (8, HALF), 0)

    def build(q, b):
        cols = half_cols(8 * q + b)
        x = XA[q, b + 1]
        pad = jnp.zeros((8, HALF), F32)
        xp = jnp.concatenate([pad, x, pad], axis=0)
        XS[0] = xp
        for shift in range(1, 8):
            XS[shift] = pltpu.roll(xp, 80 - shift, 0)

        def row(i):
            return XA[q, b + 1, i : i + 1, :]

        def half(runs):
            value = None
            for first, i, shift, base in runs:
                term = row(i) * XS[shift, base : base + 8, :]
                value = term if value is None else jnp.where(row8 >= first, term, value)
            return value

        for first, count, what in segments:
            if isinstance(what, tuple):
                value = jnp.concatenate([half(what[0]), half(what[1])], axis=0)
            else:
                i, shift, base = what
                value = row(i) * XS[shift, base : base + count, :]
            high, low = split(value)
            AH[first : first + count, cols] = high
            AL[first : first + count, cols] = low
        for n in range(8):
            for p, k in enumerate((260 * n + 128, 260 * n + 129, 260 * n + 258, 260 * n + 259)):
                i, j = pair_of(k)
                LQ[8 * n + p : 8 * n + p + 1, :] = row(i) * row(j)
        high, low = split(x)
        LH[0:64, cols] = high
        LL[0:64, cols] = low
        high, low = split(LQ[...])
        LH[128:192, cols] = high
        LL[128:192, cols] = low
        at = pl.multiple_of(8 * s, 8)
        high, low = split(jnp.concatenate([LQ[pl.ds(at, 8), :], XA[q, b + 1, pl.ds(at, 8), :]], axis=0))
        MH[256:272, cols] = high
        ML[256:272, cols] = low

    own = pl.ds(pl.multiple_of(256 * s, 256), 256)

    def build_half(q):
        cols = pl.ds(2048 * q, 2048)
        loop(0, 8, lambda b: build(q, b))
        MH[0:256, cols] = AH[own, cols]
        ML[0:256, cols] = AL[own, cols]

    def products(high, low, cols):
        out = lax.dot_general(MH[:, cols], high, ROWS_BY_ROWS, preferred_element_type=F32)
        out += lax.dot_general(ML[:, cols], high, ROWS_BY_ROWS, preferred_element_type=F32)
        return out + lax.dot_general(MH[:, cols], low, ROWS_BY_ROWS, preferred_element_type=F32)

    def chip_at(o):
        return ((y + o % 4) % 4) * 2 + (xl + o // 4) % 2

    def tile_products(t, cols):
        rows = pl.ds(pl.multiple_of(256 * chip_at(7 - t), 256), 256)
        return products(AH[rows, cols], AL[rows, cols], cols)

    loop(1, 8, lambda o: arrival(0, o).wait_recv())
    build_half(0)

    loop(1, 8, lambda o: arrival(1, o).wait_recv())

    halo = (
        copy(XA.at[1, 8, :, 128:256], XA.at[1, 0, :, 128:256], halo_s.at[0], halo_r.at[0], up, s),
        copy(XA.at[0, 1, :, 0:128], XA.at[0, 9, :, 0:128], halo_s.at[1], halo_r.at[1], down, s),
    )
    halo[0].start()
    halo[1].start()
    build_half(1)
    halo[0].wait()
    halo[1].wait()
    tail = XA[1, 0, :, 128:256]
    ghost = 2.0 * XA[0, 1, :, 0:1] - XA[0, 1, :, 1:2]
    XA[1, 0, :, 128:256] = jnp.where(a == 0, jnp.broadcast_to(ghost, (64, 128)), tail)
    head = XA[0, 9, :, 0:128]
    ghost = 2.0 * XA[1, 8, :, HALF - 1 : HALF] - XA[1, 8, :, HALF - 2 : HALF - 1]
    XA[0, 9, :, 0:128] = jnp.where(a == 15, jnp.broadcast_to(ghost, (64, 128)), head)
    lane = lax.broadcasted_iota(jnp.int32, (64, HALF), 1)

    def rates_of(q, b):
        x = XA[q, b + 1]
        before = XA[1 - q, b + q, :, HALF - 1 : HALF]
        after = XA[1 - q, b + 1 + q, :, 0:1]
        before = jnp.where(lane == 0, jnp.broadcast_to(before, x.shape), pltpu.roll(x, 1, 1))
        after = jnp.where(lane == HALF - 1, jnp.broadcast_to(after, x.shape), pltpu.roll(x, HALF - 1, 1))
        return 0.5 * (after - before)

    for q in range(2):
        def rate_rows(b):
            high, low = split(rates_of(q, b))
            LH[64:128, half_cols(8 * q + b)] = high
            LL[64:128, half_cols(8 * q + b)] = low

        loop(0, 8, rate_rows)
        rates_o[:, HALF * q : HALF * q + HALF] = rates_of(q, s)

    accl[...] = products(LH[...], LL[...], slice(0, SLAB))
    turn[0:272, :] = accl[...]
    turn[272:384, :] = jnp.zeros((112, 256), F32)
    for k in range(3):
        lines = turn[128 * k : 128 * k + 128, 0:128].T
        for t in range(16):
            lom[t % 2, t // 2, k] = lines[8 * t : 8 * t + 8, :]
        lines = turn[128 * k : 128 * k + 128, 128:256].T
        for t in range(8):
            lom[0, t, 3 + k] = lines[8 * t : 8 * t + 8, :]
            lom[1, t, 3 + k] = lines[8 * t : 8 * t + 8, :]

    def lo_pair():
        return copy(lom.at[1 - c], lomr, lc_s.at[8], lc_r.at[8], sibling, s)

    def lo_share(o):
        to = (chip + o) % 8
        return copy(lom.at[c, to], lor.at[o], lo_s.at[o], lo_r.at[o], to * 2 + c, s)

    def lo_times(o):
        part = LOT.at[chip]
        return copy(part, part, lt_s.at[o], lt_r.at[o], ((chip + o) % 8) * 2 + c, s)

    def lo_times_arrival(o):
        part = LOT.at[(chip + 8 - o) % 8]
        return copy(part, part, lt_s.at[o], lt_r.at[o], ((chip + o) % 8) * 2 + c, s)

    def lo_space(o):
        return copy(LOA.at[0, c], LOA.at[o, c], lx_s.at[o], lx_r.at[o], a, space_to(o))

    def lo_core(o):
        return copy(LOA.at[o, c], LOA.at[o, c], lc_s.at[o], lc_r.at[o], sibling, s)

    def lo_core_arrival(o):
        return copy(LOA.at[o, 1 - c], LOA.at[o, 1 - c], lc_s.at[o], lc_r.at[o], sibling, s)

    def lo_step_1():
        lo_pair().wait()
        lom[c] += lomr[...]
        loop(1, 8, lambda o: lo_share(o).start())

    def lo_step_2():
        loop(1, 8, lambda o: lo_share(o).wait_recv())
        lor[0] = lom[c, chip]
        los[...] = jnp.zeros((6, 8, 128), F32)

        def add(k):
            los[...] += lor[(chip + 8 - k) % 8]

        loop(0, 8, add)
        LOT[chip] = los[0:3]
        loop(1, 8, lambda o: lo_times(o).start())

    lane8 = lax.broadcasted_iota(jnp.int32, (8, 128), 1)

    def lo_step_3():
        loop(1, 8, lambda o: lo_times_arrival(o).wait_recv())
        packed = LOT[0, 2]
        for k in range(8):
            LOA[0, c, k] = LOT[k, 0]
            LOA[0, c, 8 + k] = LOT[k, 1]
            if k:
                packed = jnp.where(lane8 // 16 == k, pltpu.roll(LOT[k, 2], 16 * k, 1), packed)
        LOA[0, c, 16] = packed
        LOA[0, c, 17] = jnp.zeros((8, 128), F32)
        for k in range(3):
            LOA[0, c, 17, k : k + 1, :] = los[3 + k, 4:5, :]
        lo_core(0).start()
        loop(1, 8, lambda o: lo_space(o).start())

    def forward(o):
        lo_space(o).wait_recv()
        lo_core(o).start()

    lo_pair().start()

    def core_share(t):
        return copy(accs.at[t, 1 - c, 0:SENT], crecv.at[t], core_s.at[t], core_r.at[t], sibling, s)

    def y_share(o):
        to = ((y + o % 4) % 4) * 4 + xl * 2 + c
        return copy(accs.at[7 - o, c, 0:SENT], yrecv.at[o], y_s.at[o], y_r.at[o], to, s)

    def x_share():
        return copy(xsend, xrecv, x_s, x_r, y * 4 + (1 - xl) * 2 + c, s)

    def pass_on(t):
        core_share(t).wait_recv()
        accs[t, c, 0:SENT, :] += crecv[t]

        @pl.when(t % 4 < 3)
        def _():
            y_share(7 - t).start()

    def add_y(into, low):
        into[0:SENT] = accs[7 - low, c, 0:SENT, :]

        def add(o):
            y_share(o).wait_recv()
            into[0:SENT] += yrecv[o]

        loop(low + 1, low + 4, add)

    def tile(t):
        out = tile_products(t, slice(0, SLAB))
        accs[t, 0] = out[:, 0:128]
        accs[t, 1] = out[:, 128:256]
        core_share(t).start()

        @pl.when(t > 0)
        def _():
            pass_on(t - 1)

        @pl.when(t == 0)
        def _():
            lo_step_1()

        @pl.when(t == 2)
        def _():
            lo_step_2()

        @pl.when(t == 4)
        def _():
            lo_step_3()

        @pl.when(t == 6)
        def _():
            add_y(xsend, 4)
            x_share().start()

        @pl.when(t == 7)
        def _():
            loop(1, 8, forward)

    loop(0, 8, tile)
    pass_on(7)

    scale = 1.0 / (SLAB * TIMES)
    add_y(accl.at[:, 0:128], 0)
    x_share().wait_recv()
    turn[0:SENT, 0:128] = accl[0:SENT, 0:128] + xrecv[...]
    left, right, four = (turn[128 * k : 128 * k + 128, 0:128].T for k in range(3))

    def place(left, right, four):
        low = lax.broadcasted_iota(jnp.int32, left.shape, 1) < 2
        moved = pltpu.roll(right, 2, 1)
        return left, jnp.where(low, four, moved), jnp.where(low, moved, four)

    first, second, third = place(left, right, four)
    gram_o[0:128, 0:128] = first * scale
    gram_o[0:128, 128:256] = second * scale
    gram_o[0:128, 256:260] = third[:, 0:4] * scale
    parts = place(los[3], los[4], los[5])
    first, second, third = (jnp.where(c == 0, part[0:2, :], part[2:4, :]) * scale for part in parts)
    gram_o[128:130, 0:128] = first
    gram_o[128:130, 128:256] = second
    gram_o[128:130, 256:260] = third[:, 0:4]

    loop(0, 8, lambda o: lo_core_arrival(o).wait_recv())

    wide = lax.broadcasted_iota(jnp.int32, (136, 128), 1)
    carried = jnp.zeros((136, 128), F32)
    last = jnp.zeros((136, 128), F32)
    for b in range(8):
        o = ((xh + 2 - b // 4) % 2) * 4 + (z + 4 - b % 4) % 4
        ones = LOA[o, 0, 17]
        left = jnp.concatenate([LOA[o, t % 2, t // 2] for t in range(16)] + [ones], axis=0)
        right = jnp.concatenate([LOA[o, t % 2, 8 + t // 2] for t in range(16)] + [pltpu.roll(ones, 7, 0)], axis=0)
        packed = [LOA[o, t, 16] for t in range(2)]
        four = jnp.concatenate(
            [pltpu.roll(packed[t % 2], (128 - 16 * (t // 2)) % 128, 1) if t // 2 else packed[t % 2] for t in range(16)]
            + [pltpu.roll(ones, 6, 0)],
            axis=0,
        )
        shift = 4 * b
        first, second, third = (pltpu.roll(v, shift, 1) if b else v for v in place(left, right, four))
        GS[:, 256 * b : 256 * b + 128] = jnp.where(wide < shift, carried, first)
        GS[:, 256 * b + 128 : 256 * b + 256] = jnp.where(wide < shift, first, second)
        carried = jnp.where(wide < shift, second, third)
        modes = pltpu.roll(four, 25 + 8 * b, 1)
        last = jnp.where((wide >= 33 + 8 * b) & (wide < 41 + 8 * b), modes, last)
        if b == 7:
            last = jnp.where(wide == 32, pltpu.roll(four, 28, 1), last)
    GS[:, 2048:2176] = jnp.where(wide < 32, carried, last)
    side_o[0:1, :] = GS[128:129, 0:2145] * scale
    side_o[1:65, :] = GS[0:64, 0:2145] * scale
    rhs_o[...] = GS[64:128, 0:2145] * scale

    for q in range(2):
        loop(1, 8, lambda o: share(q, o).wait_send())
        loop(1, 8, lambda o: spread(q, o).wait_send())
    loop(1, 8, lambda o: lo_share(o).wait_send())
    loop(1, 8, lambda o: lo_times(o).wait_send())
    loop(1, 8, lambda o: lo_space(o).wait_send())
    loop(0, 8, lambda o: lo_core(o).wait_send())
    loop(0, 8, lambda t: core_share(t).wait_send())
    loop(1, 4, lambda o: y_share(o).wait_send())
    loop(5, 8, lambda o: y_share(o).wait_send())
    x_share().wait_send()


def hand_over_kernel(*refs):
    count = len(refs) // 2
    for given, final in zip(refs[:count], refs[count:]):
        final[...] = given[...]


def hand_over(*arrays):
    vmem = pl.BlockSpec(memory_space=pltpu.VMEM)
    return pl.pallas_call(
        hand_over_kernel,
        out_shape=tuple(jax.ShapeDtypeStruct(each.shape, each.dtype) for each in arrays),
        in_specs=[vmem] * len(arrays),
        out_specs=(vmem,) * len(arrays),
        compiler_params=pltpu.CompilerParams(vmem_limit_bytes=16 << 20),
    )(*arrays)


def body(snapshots, basis):
    vmem = pl.BlockSpec(memory_space=pltpu.VMEM)
    dma = pltpu.SemaphoreType.DMA
    rates, gram_quad, gram_side, rhs = pl.pallas_call(
        kernel,
        out_shape=(
            jax.ShapeDtypeStruct((MODES, BLOCK), F32),
            jax.ShapeDtypeStruct((130, 260), F32),
            jax.ShapeDtypeStruct((65, 2145), F32),
            jax.ShapeDtypeStruct((64, 2145), F32),
        ),
        in_specs=[pl.BlockSpec(memory_space=pl.ANY), vmem],
        out_specs=(vmem, vmem, vmem, vmem),
        scratch_shapes=[
            pltpu.VMEM((2048, SLAB), BF16),
            pltpu.VMEM((2048, SLAB), BF16),
            pltpu.VMEM((MINE, SLAB), BF16),
            pltpu.VMEM((MINE, SLAB), BF16),
            pltpu.VMEM((256, SLAB), BF16),
            pltpu.VMEM((256, SLAB), BF16),
            pltpu.VMEM((2, 10, MODES, HALF), F32),
            pltpu.VMEM((8, 80, HALF), F32),
            pltpu.VMEM((64, HALF), F32),
            pltpu.VMEM((16, MODES, HALF), F32),
            pltpu.VMEM((16, MODES, HALF), F32),
            pltpu.VMEM((8, 2, MINE, 128), F32),
            pltpu.VMEM((8, SENT, 128), F32),
            pltpu.VMEM((8, SENT, 128), F32),
            pltpu.VMEM((SENT, 128), F32),
            pltpu.VMEM((SENT, 128), F32),
            pltpu.VMEM((MINE, 256), F32),
            pltpu.VMEM((384, 256), F32),
            pltpu.VMEM((2, 8, 6, 8, 128), F32),
            pltpu.VMEM((8, 6, 8, 128), F32),
            pltpu.VMEM((8, 6, 8, 128), F32),
            pltpu.VMEM((6, 8, 128), F32),
            pltpu.VMEM((8, 3, 8, 128), F32),
            pltpu.VMEM((8, 2, 18, 8, 128), F32),
            pltpu.VMEM((136, 2176), F32),
            dma((16,)), dma((16,)), dma((16,)), dma((16,)), dma((16,)), dma((2,)), dma((2,)),
            dma((8,)), dma((8,)), dma((8,)), dma((8,)), dma(()), dma(()),
            dma((8,)), dma((8,)), dma((8,)), dma((8,)), dma((8,)), dma((8,)), dma((9,)), dma((9,)),
        ],
        compiler_params=pltpu.CompilerParams(
            collective_id=0, has_side_effects=True, vmem_limit_bytes=60 << 20
        ),
    )(snapshots, basis.T)
    rates, gram_quad, gram_side, rhs = hand_over(rates, gram_quad, gram_side, rhs)
    return rates, gram_quad, gram_side, rhs.T


def solution(mesh):
    in_specs = (P("space", "tm"), P("space", None))
    out_specs = (P(None, ("tm", "space")), P("tm", "space"), P(), P())
    return jax.shard_map(body, mesh=mesh, in_specs=in_specs, out_specs=out_specs, check_vma=False)
```

```python
import functools

import jax
import jax.numpy as jnp
import numpy as np
from jax import lax
from jax.experimental import pallas as pl
from jax.experimental.pallas import tpu as pltpu
from jax.sharding import PartitionSpec as P

F32 = jnp.float32
BF16 = jnp.bfloat16
MESH = pl.DeviceIdType.MESH
ROWS_BY_ROWS = (((1,), (1,)), ((), ()))

MODES = 64
SPACE = 8
TIMES = 16
BLOCK = 512
HALF = 256
SLAB = SPACE * BLOCK
MINE = 272
SENT = 264


def pair_of(k):
    i = 0
    while k >= MODES - i:
        k -= MODES - i
        i += 1
    return i, i + k


def half_plan(row):
    block, inside = divmod(row, 128)
    runs = []
    for r in range(8):
        i, j = pair_of(130 * block + inside + r)
        if not runs or runs[-1][1] != i:
            at = j - r + 8
            runs.append((r, i, at % 8, at - at % 8))
    return runs


def build_plan():
    segments = []
    for row in range(0, 2048, 16):
        low, high = half_plan(row), half_plan(row + 8)
        pure = len(low) == 1 and len(high) == 1 and low[0][1:3] == high[0][1:3]
        if not pure:
            segments.append((row, 16, (low, high)))
            continue
        run = low[0]
        last = segments[-1] if segments else None
        if (
            last
            and not isinstance(last[2], tuple)
            and last[2][0] == list(run)[1]
            and last[2][1] == run[2]
            and last[2][2] + last[1] == run[3]
        ):
            segments[-1] = (last[0], last[1] + 16, last[2])
        else:
            segments.append((row, 16, [run[1], run[2], run[3]]))
    return segments


def kernel(
    snap, basis, rates_o, gram_o, side_o, rhs_o,
    AH, AL, MH, ML, LH, LL, XA, XS, LQ, sbuf, rbuf, accs, crecv, yrecv, xsend, xrecv,
    accl, turn, lom, lomr, lor, los, LOT, LOA, GS,
    snap_sem, rs_s, rs_r, ag_s, ag_r, halo_s, halo_r, core_s, core_r, y_s, y_r, x_s, x_r,
    lo_s, lo_r, lt_s, lt_r, lx_s, lx_r, lc_s, lc_r,
):
    a = lax.axis_index("tm")
    s = lax.axis_index("space")
    y, xl, c = a // 4, (a // 2) % 2, a % 2
    chip = a // 2
    sibling = a + 1 - 2 * c
    xh, z = s // 4, s % 4

    def space_to(o):
        return ((xh + o // 4) % 2) * 4 + (z + o % 4) % 4

    def space_from(o):
        return ((xh + 2 - o // 4) % 2) * 4 + (z + 4 - o % 4) % 4

    def copy(src, dst, ss, rs, tm, sp):
        return pltpu.make_async_remote_copy(
            src_ref=src, dst_ref=dst, send_sem=ss, recv_sem=rs, device_id=(tm, sp), device_id_type=MESH
        )

    def loop(low, high, step):
        def inner(k, carry):
            step(k)
            return carry

        lax.fori_loop(low, high, inner, 0)

    def half_cols(m):
        return pl.ds(pl.multiple_of(HALF * m, HALF), HALF)

    def fetch(m):
        cols = pl.ds(pl.multiple_of(BLOCK * space_to(7 - m % 8) + HALF * (m // 8), HALF), HALF)
        return pltpu.make_async_copy(snap.at[:, cols], AH.at[:, half_cols(m)], snap_sem.at[m])

    loop(0, 8, lambda m: fetch(m).start())

    barrier = pltpu.get_barrier_semaphore()

    def greet(tm, sp):
        pl.semaphore_signal(barrier, inc=1, device_id=(tm, sp), device_id_type=MESH)

    up, down = (a + 1) % 16, (a + 15) % 16
    loop(1, 8, lambda o: greet(a, space_to(o)))
    loop(1, 8, lambda o: greet(((chip + o) % 8) * 2 + c, s))
    greet(sibling, s)
    greet(up, s)
    greet(down, s)

    loop(8, 16, lambda m: fetch(m).start())

    def project(m):
        fetch(m).wait()
        sbuf[m] = jnp.dot(basis[...], AH[:, half_cols(m)], preferred_element_type=F32)

    def share(q, o):
        at = 8 * q + o
        return copy(sbuf.at[8 * q + 7 - o], rbuf.at[at], rs_s.at[at], rs_r.at[at], a, space_to(o))

    loop(0, 8, project)
    pl.semaphore_wait(barrier, 17)
    loop(0, 7, lambda m: share(0, 7 - m).start())

    def middle(m):
        project(m)

        @pl.when(m < 15)
        def _():
            share(1, 15 - m).start()

    loop(8, 16, middle)

    def spread(q, o):
        mine = XA.at[q, s + 1]
        return copy(mine, mine, ag_s.at[8 * q + o], ag_r.at[8 * q + o], a, space_to(o))

    def arrival(q, o):
        theirs = XA.at[q, space_from(o) + 1]
        return copy(theirs, theirs, ag_s.at[8 * q + o], ag_r.at[8 * q + o], a, space_to(o))

    for q in range(2):
        def add_share(o):
            share(q, o).wait_recv()
            sbuf[8 * q + 7] += rbuf[8 * q + o]

        loop(1, 8, add_share)
        XA[q, s + 1] = sbuf[8 * q + 7]
        loop(1, 8, lambda o: spread(q, o).start())

    segments = build_plan()

    def split(value):
        high = value.astype(BF16)
        return high, (value - high.astype(F32)).astype(BF16)

    LQ[...] = jnp.where(lax.broadcasted_iota(jnp.int32, (64, HALF), 0) % 8 == 4, 1.0, 0.0).astype(F32)
    LH[192:256, :] = jnp.zeros((64, SLAB), BF16)
    LL[192:256, :] = jnp.zeros((64, SLAB), BF16)
    row8 = lax.broadcasted_iota(jnp.int32, (8, HALF), 0)

    def build(q, b):
        cols = half_cols(8 * q + b)
        x = XA[q, b + 1]
        pad = jnp.zeros((8, HALF), F32)
        xp = jnp.concatenate([pad, x, pad], axis=0)
        XS[0] = xp
        for shift in range(1, 8):
            XS[shift] = pltpu.roll(xp, 80 - shift, 0)

        def row(i):
            return XA[q, b + 1, i : i + 1, :]

        def half(runs):
            value = None
            for first, i, shift, base in runs:
                term = row(i) * XS[shift, base : base + 8, :]
                value = term if value is None else jnp.where(row8 >= first, term, value)
            return value

        for first, count, what in segments:
            if isinstance(what, tuple):
                value = jnp.concatenate([half(what[0]), half(what[1])], axis=0)
            else:
                i, shift, base = what
                value = row(i) * XS[shift, base : base + count, :]
            high, low = split(value)
            AH[first : first + count, cols] = high
            AL[first : first + count, cols] = low
        for n in range(8):
            for p, k in enumerate((260 * n + 128, 260 * n + 129, 260 * n + 258, 260 * n + 259)):
                i, j = pair_of(k)
                LQ[8 * n + p : 8 * n + p + 1, :] = row(i) * row(j)
        high, low = split(x)
        LH[0:64, cols] = high
        LL[0:64, cols] = low
        high, low = split(LQ[...])
        LH[128:192, cols] = high
        LL[128:192, cols] = low
        at = pl.multiple_of(8 * s, 8)
        high, low = split(jnp.concatenate([LQ[pl.ds(at, 8), :], XA[q, b + 1, pl.ds(at, 8), :]], axis=0))
        MH[256:272, cols] = high
        ML[256:272, cols] = low

    own = pl.ds(pl.multiple_of(256 * s, 256), 256)

    def build_half(q):
        cols = pl.ds(2048 * q, 2048)
        loop(0, 8, lambda b: build(q, b))
        MH[0:256, cols] = AH[own, cols]
        ML[0:256, cols] = AL[own, cols]

    def products(high, low, cols):
        out = lax.dot_general(MH[:, cols], high, ROWS_BY_ROWS, preferred_element_type=F32)
        out += lax.dot_general(ML[:, cols], high, ROWS_BY_ROWS, preferred_element_type=F32)
        return out + lax.dot_general(MH[:, cols], low, ROWS_BY_ROWS, preferred_element_type=F32)

    def chip_at(o):
        return ((y + o % 4) % 4) * 2 + (xl + o // 4) % 2

    def tile_products(t, cols):
        rows = pl.ds(pl.multiple_of(256 * chip_at(7 - t), 256), 256)
        return products(AH[rows, cols], AL[rows, cols], cols)

    loop(1, 8, lambda o: arrival(0, o).wait_recv())
    build_half(0)

    loop(1, 8, lambda o: arrival(1, o).wait_recv())

    halo = (
        copy(XA.at[1, 8, :, 128:256], XA.at[1, 0, :, 128:256], halo_s.at[0], halo_r.at[0], up, s),
        copy(XA.at[0, 1, :, 0:128], XA.at[0, 9, :, 0:128], halo_s.at[1], halo_r.at[1], down, s),
    )
    halo[0].start()
    halo[1].start()
    build_half(1)
    halo[0].wait()
    halo[1].wait()
    tail = XA[1, 0, :, 128:256]
    ghost = 2.0 * XA[0, 1, :, 0:1] - XA[0, 1, :, 1:2]
    XA[1, 0, :, 128:256] = jnp.where(a == 0, jnp.broadcast_to(ghost, (64, 128)), tail)
    head = XA[0, 9, :, 0:128]
    ghost = 2.0 * XA[1, 8, :, HALF - 1 : HALF] - XA[1, 8, :, HALF - 2 : HALF - 1]
    XA[0, 9, :, 0:128] = jnp.where(a == 15, jnp.broadcast_to(ghost, (64, 128)), head)
    lane = lax.broadcasted_iota(jnp.int32, (64, HALF), 1)

    def rates_of(q, b):
        x = XA[q, b + 1]
        before = XA[1 - q, b + q, :, HALF - 1 : HALF]
        after = XA[1 - q, b + 1 + q, :, 0:1]
        before = jnp.where(lane == 0, jnp.broadcast_to(before, x.shape), pltpu.roll(x, 1, 1))
        after = jnp.where(lane == HALF - 1, jnp.broadcast_to(after, x.shape), pltpu.roll(x, HALF - 1, 1))
        return 0.5 * (after - before)

    for q in range(2):
        def rate_rows(b):
            high, low = split(rates_of(q, b))
            LH[64:128, half_cols(8 * q + b)] = high
            LL[64:128, half_cols(8 * q + b)] = low

        loop(0, 8, rate_rows)
        rates_o[:, HALF * q : HALF * q + HALF] = rates_of(q, s)

    accl[...] = products(LH[...], LL[...], slice(0, SLAB))
    turn[0:272, :] = accl[...]
    turn[272:384, :] = jnp.zeros((112, 256), F32)
    for k in range(3):
        lines = turn[128 * k : 128 * k + 128, 0:128].T
        for t in range(16):
            lom[t % 2, t // 2, k] = lines[8 * t : 8 * t + 8, :]
        lines = turn[128 * k : 128 * k + 128, 128:256].T
        for t in range(8):
            lom[0, t, 3 + k] = lines[8 * t : 8 * t + 8, :]
            lom[1, t, 3 + k] = lines[8 * t : 8 * t + 8, :]

    def lo_pair():
        return copy(lom.at[1 - c], lomr, lc_s.at[8], lc_r.at[8], sibling, s)

    def lo_share(o):
        to = (chip + o) % 8
        return copy(lom.at[c, to], lor.at[o], lo_s.at[o], lo_r.at[o], to * 2 + c, s)

    def lo_times(o):
        part = LOT.at[chip]
        return copy(part, part, lt_s.at[o], lt_r.at[o], ((chip + o) % 8) * 2 + c, s)

    def lo_times_arrival(o):
        part = LOT.at[(chip + 8 - o) % 8]
        return copy(part, part, lt_s.at[o], lt_r.at[o], ((chip + o) % 8) * 2 + c, s)

    def lo_space(o):
        return copy(LOA.at[0, c], LOA.at[o, c], lx_s.at[o], lx_r.at[o], a, space_to(o))

    def lo_core(o):
        return copy(LOA.at[o, c], LOA.at[o, c], lc_s.at[o], lc_r.at[o], sibling, s)

    def lo_core_arrival(o):
        return copy(LOA.at[o, 1 - c], LOA.at[o, 1 - c], lc_s.at[o], lc_r.at[o], sibling, s)

    def lo_step_1():
        lo_pair().wait()
        lom[c] += lomr[...]
        loop(1, 8, lambda o: lo_share(o).start())

    def lo_step_2():
        loop(1, 8, lambda o: lo_share(o).wait_recv())
        lor[0] = lom[c, chip]
        los[...] = jnp.zeros((6, 8, 128), F32)

        def add(k):
            los[...] += lor[(chip + 8 - k) % 8]

        loop(0, 8, add)
        LOT[chip] = los[0:3]
        loop(1, 8, lambda o: lo_times(o).start())

    lane8 = lax.broadcasted_iota(jnp.int32, (8, 128), 1)

    def lo_step_3():
        loop(1, 8, lambda o: lo_times_arrival(o).wait_recv())
        packed = LOT[0, 2]
        for k in range(8):
            LOA[0, c, k] = LOT[k, 0]
            LOA[0, c, 8 + k] = LOT[k, 1]
            if k:
                packed = jnp.where(lane8 // 16 == k, pltpu.roll(LOT[k, 2], 16 * k, 1), packed)
        LOA[0, c, 16] = packed
        LOA[0, c, 17] = jnp.zeros((8, 128), F32)
        for k in range(3):
            LOA[0, c, 17, k : k + 1, :] = los[3 + k, 4:5, :]
        lo_core(0).start()
        loop(1, 8, lambda o: lo_space(o).start())

    def forward(o):
        lo_space(o).wait_recv()
        lo_core(o).start()

    lo_pair().start()

    def core_share(t):
        return copy(accs.at[t, 1 - c, 0:SENT], crecv.at[t], core_s.at[t], core_r.at[t], sibling, s)

    def y_share(o):
        to = ((y + o % 4) % 4) * 4 + xl * 2 + c
        return copy(accs.at[7 - o, c, 0:SENT], yrecv.at[o], y_s.at[o], y_r.at[o], to, s)

    def x_share():
        return copy(xsend, xrecv, x_s, x_r, y * 4 + (1 - xl) * 2 + c, s)

    def pass_on(t):
        core_share(t).wait_recv()
        accs[t, c, 0:SENT, :] += crecv[t]

        @pl.when(t % 4 < 3)
        def _():
            y_share(7 - t).start()

    def add_y(into, low):
        into[0:SENT] = accs[7 - low, c, 0:SENT, :]

        def add(o):
            y_share(o).wait_recv()
            into[0:SENT] += yrecv[o]

        loop(low + 1, low + 4, add)

    def tile(t):
        out = tile_products(t, slice(0, SLAB))
        accs[t, 0] = out[:, 0:128]
        accs[t, 1] = out[:, 128:256]
        core_share(t).start()

        @pl.when(t > 0)
        def _():
            pass_on(t - 1)

        @pl.when(t == 0)
        def _():
            lo_step_1()

        @pl.when(t == 2)
        def _():
            lo_step_2()

        @pl.when(t == 4)
        def _():
            lo_step_3()

        @pl.when(t == 6)
        def _():
            add_y(xsend, 4)
            x_share().start()

        @pl.when(t == 7)
        def _():
            loop(1, 8, forward)

    loop(0, 8, tile)
    pass_on(7)

    scale = 1.0 / (SLAB * TIMES)
    add_y(accl.at[:, 0:128], 0)
    x_share().wait_recv()
    turn[0:SENT, 0:128] = accl[0:SENT, 0:128] + xrecv[...]
    left, right, four = (turn[128 * k : 128 * k + 128, 0:128].T for k in range(3))

    def place(left, right, four):
        low = lax.broadcasted_iota(jnp.int32, left.shape, 1) < 2
        moved = pltpu.roll(right, 2, 1)
        return left, jnp.where(low, four, moved), jnp.where(low, moved, four)

    first, second, third = place(left, right, four)
    gram_o[0:128, 0:128] = first * scale
    gram_o[0:128, 128:256] = second * scale
    gram_o[0:128, 256:260] = third[:, 0:4] * scale
    parts = place(los[3], los[4], los[5])
    first, second, third = (jnp.where(c == 0, part[0:2, :], part[2:4, :]) * scale for part in parts)
    gram_o[128:130, 0:128] = first
    gram_o[128:130, 128:256] = second
    gram_o[128:130, 256:260] = third[:, 0:4]

    loop(0, 8, lambda o: lo_core_arrival(o).wait_recv())

    wide = lax.broadcasted_iota(jnp.int32, (136, 128), 1)
    carried = jnp.zeros((136, 128), F32)
    last = jnp.zeros((136, 128), F32)
    for b in range(8):
        o = ((xh + 2 - b // 4) % 2) * 4 + (z + 4 - b % 4) % 4
        ones = LOA[o, 0, 17]
        left = jnp.concatenate([LOA[o, t % 2, t // 2] for t in range(16)] + [ones], axis=0)
        right = jnp.concatenate([LOA[o, t % 2, 8 + t // 2] for t in range(16)] + [pltpu.roll(ones, 7, 0)], axis=0)
        packed = [LOA[o, t, 16] for t in range(2)]
        four = jnp.concatenate(
            [pltpu.roll(packed[t % 2], (128 - 16 * (t // 2)) % 128, 1) if t // 2 else packed[t % 2] for t in range(16)]
            + [pltpu.roll(ones, 6, 0)],
            axis=0,
        )
        shift = 4 * b
        first, second, third = (pltpu.roll(v, shift, 1) if b else v for v in place(left, right, four))
        GS[:, 256 * b : 256 * b + 128] = jnp.where(wide < shift, carried, first)
        GS[:, 256 * b + 128 : 256 * b + 256] = jnp.where(wide < shift, first, second)
        carried = jnp.where(wide < shift, second, third)
        modes = pltpu.roll(four, 25 + 8 * b, 1)
        last = jnp.where((wide >= 33 + 8 * b) & (wide < 41 + 8 * b), modes, last)
        if b == 7:
            last = jnp.where(wide == 32, pltpu.roll(four, 28, 1), last)
    GS[:, 2048:2176] = jnp.where(wide < 32, carried, last)
    side_o[0:1, :] = GS[128:129, 0:2145] * scale
    side_o[1:65, :] = GS[0:64, 0:2145] * scale
    rhs_o[...] = GS[64:128, 0:2145] * scale

    for q in range(2):
        loop(1, 8, lambda o: share(q, o).wait_send())
        loop(1, 8, lambda o: spread(q, o).wait_send())
    loop(1, 8, lambda o: lo_share(o).wait_send())
    loop(1, 8, lambda o: lo_times(o).wait_send())
    loop(1, 8, lambda o: lo_space(o).wait_send())
    loop(0, 8, lambda o: lo_core(o).wait_send())
    loop(0, 8, lambda t: core_share(t).wait_send())
    loop(1, 4, lambda o: y_share(o).wait_send())
    loop(5, 8, lambda o: y_share(o).wait_send())
    x_share().wait_send()


def hand_over_kernel(*refs):
    count = (len(refs) - 2) // 3
    given, final, held = refs[:count], refs[count : 2 * count], refs[2 * count : 3 * count]
    come, go = refs[-2:]
    arrive = [pltpu.make_async_copy(given[k], held[k], come.at[k]) for k in range(count)]
    leave = [pltpu.make_async_copy(held[k], final[k], go.at[k]) for k in range(count)]
    for each in arrive:
        each.start()
    for k in range(count):
        arrive[k].wait()
        leave[k].start()
    for each in leave:
        each.wait()


def hand_over(*arrays):
    anywhere = pl.BlockSpec(memory_space=pl.ANY)
    return pl.pallas_call(
        hand_over_kernel,
        out_shape=tuple(jax.ShapeDtypeStruct(each.shape, each.dtype) for each in arrays),
        in_specs=[anywhere] * len(arrays),
        out_specs=(anywhere,) * len(arrays),
        scratch_shapes=[pltpu.VMEM(each.shape, each.dtype) for each in arrays]
        + [pltpu.SemaphoreType.DMA((len(arrays),))] * 2,
        compiler_params=pltpu.CompilerParams(vmem_limit_bytes=60 << 20),
    )(*arrays)


def body(snapshots, basis):
    vmem = pl.BlockSpec(memory_space=pltpu.VMEM)
    dma = pltpu.SemaphoreType.DMA
    rates, gram_quad, gram_side, rhs = pl.pallas_call(
        kernel,
        out_shape=(
            jax.ShapeDtypeStruct((MODES, BLOCK), F32),
            jax.ShapeDtypeStruct((130, 260), F32),
            jax.ShapeDtypeStruct((65, 2145), F32),
            jax.ShapeDtypeStruct((64, 2145), F32),
        ),
        in_specs=[pl.BlockSpec(memory_space=pl.ANY), vmem],
        out_specs=(vmem, vmem, vmem, vmem),
        scratch_shapes=[
            pltpu.VMEM((2048, SLAB), BF16),
            pltpu.VMEM((2048, SLAB), BF16),
            pltpu.VMEM((MINE, SLAB), BF16),
            pltpu.VMEM((MINE, SLAB), BF16),
            pltpu.VMEM((256, SLAB), BF16),
            pltpu.VMEM((256, SLAB), BF16),
            pltpu.VMEM((2, 10, MODES, HALF), F32),
            pltpu.VMEM((8, 80, HALF), F32),
            pltpu.VMEM((64, HALF), F32),
            pltpu.VMEM((16, MODES, HALF), F32),
            pltpu.VMEM((16, MODES, HALF), F32),
            pltpu.VMEM((8, 2, MINE, 128), F32),
            pltpu.VMEM((8, SENT, 128), F32),
            pltpu.VMEM((8, SENT, 128), F32),
            pltpu.VMEM((SENT, 128), F32),
            pltpu.VMEM((SENT, 128), F32),
            pltpu.VMEM((MINE, 256), F32),
            pltpu.VMEM((384, 256), F32),
            pltpu.VMEM((2, 8, 6, 8, 128), F32),
            pltpu.VMEM((8, 6, 8, 128), F32),
            pltpu.VMEM((8, 6, 8, 128), F32),
            pltpu.VMEM((6, 8, 128), F32),
            pltpu.VMEM((8, 3, 8, 128), F32),
            pltpu.VMEM((8, 2, 18, 8, 128), F32),
            pltpu.VMEM((136, 2176), F32),
            dma((16,)), dma((16,)), dma((16,)), dma((16,)), dma((16,)), dma((2,)), dma((2,)),
            dma((8,)), dma((8,)), dma((8,)), dma((8,)), dma(()), dma(()),
            dma((8,)), dma((8,)), dma((8,)), dma((8,)), dma((8,)), dma((8,)), dma((9,)), dma((9,)),
        ],
        compiler_params=pltpu.CompilerParams(
            collective_id=0, has_side_effects=True, vmem_limit_bytes=60 << 20
        ),
    )(snapshots, basis.T)
    rates, gram_quad, gram_side, rhs = hand_over(rates, gram_quad, gram_side, rhs)
    return rates, gram_quad, gram_side, rhs.T


def solution(mesh):
    in_specs = (P("space", "tm"), P("space", None))
    out_specs = (P(None, ("tm", "space")), P("tm", "space"), P(), P())
    return jax.shard_map(body, mesh=mesh, in_specs=in_specs, out_specs=out_specs, check_vma=False)
```

```python
import functools

import jax
import jax.numpy as jnp
import numpy as np
from jax import lax
from jax.experimental import pallas as pl
from jax.experimental.pallas import tpu as pltpu
from jax.sharding import PartitionSpec as P

F32 = jnp.float32
BF16 = jnp.bfloat16
MESH = pl.DeviceIdType.MESH
ROWS_BY_ROWS = (((1,), (1,)), ((), ()))

MODES = 64
SPACE = 8
TIMES = 16
BLOCK = 512
HALF = 256
SLAB = SPACE * BLOCK
MINE = 272
SENT = 264


def pair_of(k):
    i = 0
    while k >= MODES - i:
        k -= MODES - i
        i += 1
    return i, i + k


def half_plan(row):
    block, inside = divmod(row, 128)
    runs = []
    for r in range(8):
        i, j = pair_of(130 * block + inside + r)
        if not runs or runs[-1][1] != i:
            at = j - r + 8
            runs.append((r, i, at % 8, at - at % 8))
    return runs


def build_plan():
    segments = []
    for row in range(0, 2048, 16):
        low, high = half_plan(row), half_plan(row + 8)
        pure = len(low) == 1 and len(high) == 1 and low[0][1:3] == high[0][1:3]
        if not pure:
            segments.append((row, 16, (low, high)))
            continue
        run = low[0]
        last = segments[-1] if segments else None
        if (
            last
            and not isinstance(last[2], tuple)
            and last[2][0] == list(run)[1]
            and last[2][1] == run[2]
            and last[2][2] + last[1] == run[3]
        ):
            segments[-1] = (last[0], last[1] + 16, last[2])
        else:
            segments.append((row, 16, [run[1], run[2], run[3]]))
    return segments


def kernel(
    snap, basis, rates_o, gram_o, side_o, rhs_o,
    AH, AL, MH, ML, LH, LL, XA, XS, LQ, sbuf, rbuf, accs, crecv, yrecv, xsend, xrecv,
    accl, turn, lom, lomr, lor, los, LOT, LOA, GS,
    snap_sem, rs_s, rs_r, ag_s, ag_r, halo_s, halo_r, core_s, core_r, y_s, y_r, x_s, x_r,
    lo_s, lo_r, lt_s, lt_r, lx_s, lx_r, lc_s, lc_r,
):
    a = lax.axis_index("tm")
    s = lax.axis_index("space")
    y, xl, c = a // 4, (a // 2) % 2, a % 2
    chip = a // 2
    sibling = a + 1 - 2 * c
    xh, z = s // 4, s % 4

    def space_to(o):
        return ((xh + o // 4) % 2) * 4 + (z + o % 4) % 4

    def space_from(o):
        return ((xh + 2 - o // 4) % 2) * 4 + (z + 4 - o % 4) % 4

    def copy(src, dst, ss, rs, tm, sp):
        return pltpu.make_async_remote_copy(
            src_ref=src, dst_ref=dst, send_sem=ss, recv_sem=rs, device_id=(tm, sp), device_id_type=MESH
        )

    def loop(low, high, step):
        def inner(k, carry):
            step(k)
            return carry

        lax.fori_loop(low, high, inner, 0)

    def half_cols(m):
        return pl.ds(pl.multiple_of(HALF * m, HALF), HALF)

    def fetch(m):
        cols = pl.ds(pl.multiple_of(BLOCK * space_to(7 - m % 8) + HALF * (m // 8), HALF), HALF)
        return pltpu.make_async_copy(snap.at[:, cols], AH.at[:, half_cols(m)], snap_sem.at[m])

    loop(0, 8, lambda m: fetch(m).start())

    barrier = pltpu.get_barrier_semaphore()

    def greet(tm, sp):
        pl.semaphore_signal(barrier, inc=1, device_id=(tm, sp), device_id_type=MESH)

    up, down = (a + 1) % 16, (a + 15) % 16
    loop(1, 8, lambda o: greet(a, space_to(o)))
    loop(1, 8, lambda o: greet(((chip + o) % 8) * 2 + c, s))
    greet(up, s)
    greet(down, s)

    loop(8, 16, lambda m: fetch(m).start())

    def project(m):
        fetch(m).wait()
        sbuf[m] = jnp.dot(basis[...], AH[:, half_cols(m)], preferred_element_type=F32)

    def share(q, o):
        at = 8 * q + o
        return copy(sbuf.at[8 * q + 7 - o], rbuf.at[at], rs_s.at[at], rs_r.at[at], a, space_to(o))

    loop(0, 8, project)
    pl.semaphore_wait(barrier, 16)
    loop(0, 7, lambda m: share(0, 7 - m).start())

    def middle(m):
        project(m)

        @pl.when(m < 15)
        def _():
            share(1, 15 - m).start()

    loop(8, 16, middle)

    def spread(q, o):
        mine = XA.at[q, s + 1]
        return copy(mine, mine, ag_s.at[8 * q + o], ag_r.at[8 * q + o], a, space_to(o))

    def arrival(q, o):
        theirs = XA.at[q, space_from(o) + 1]
        return copy(theirs, theirs, ag_s.at[8 * q + o], ag_r.at[8 * q + o], a, space_to(o))

    for q in range(2):
        def add_share(o):
            share(q, o).wait_recv()
            sbuf[8 * q + 7] += rbuf[8 * q + o]

        loop(1, 8, add_share)
        XA[q, s + 1] = sbuf[8 * q + 7]
        loop(1, 8, lambda o: spread(q, o).start())

    segments = build_plan()

    def split(value):
        high = value.astype(BF16)
        return high, (value - high.astype(F32)).astype(BF16)

    LQ[...] = jnp.where(lax.broadcasted_iota(jnp.int32, (64, HALF), 0) % 8 == 4, 1.0, 0.0).astype(F32)
    LH[192:256, :] = jnp.zeros((64, SLAB), BF16)
    LL[192:256, :] = jnp.zeros((64, SLAB), BF16)
    row8 = lax.broadcasted_iota(jnp.int32, (8, HALF), 0)

    def build(q, b):
        cols = half_cols(8 * q + b)
        x = XA[q, b + 1]
        pad = jnp.zeros((8, HALF), F32)
        xp = jnp.concatenate([pad, x, pad], axis=0)
        XS[0] = xp
        for shift in range(1, 8):
            XS[shift] = pltpu.roll(xp, 80 - shift, 0)

        def row(i):
            return XA[q, b + 1, i : i + 1, :]

        def half(runs):
            value = None
            for first, i, shift, base in runs:
                term = row(i) * XS[shift, base : base + 8, :]
                value = term if value is None else jnp.where(row8 >= first, term, value)
            return value

        for first, count, what in segments:
            if isinstance(what, tuple):
                value = jnp.concatenate([half(what[0]), half(what[1])], axis=0)
            else:
                i, shift, base = what
                value = row(i) * XS[shift, base : base + count, :]
            high, low = split(value)
            AH[first : first + count, cols] = high
            AL[first : first + count, cols] = low
        for n in range(8):
            for p, k in enumerate((260 * n + 128, 260 * n + 129, 260 * n + 258, 260 * n + 259)):
                i, j = pair_of(k)
                LQ[8 * n + p : 8 * n + p + 1, :] = row(i) * row(j)
        high, low = split(x)
        LH[0:64, cols] = high
        LL[0:64, cols] = low
        high, low = split(LQ[...])
        LH[128:192, cols] = high
        LL[128:192, cols] = low
        at = pl.multiple_of(8 * s, 8)
        high, low = split(jnp.concatenate([LQ[pl.ds(at, 8), :], XA[q, b + 1, pl.ds(at, 8), :]], axis=0))
        MH[256:272, cols] = high
        ML[256:272, cols] = low

    own = pl.ds(pl.multiple_of(256 * s, 256), 256)

    def build_half(q):
        cols = pl.ds(2048 * q, 2048)
        loop(0, 8, lambda b: build(q, b))
        MH[0:256, cols] = AH[own, cols]
        ML[0:256, cols] = AL[own, cols]

    def products(high, low, cols):
        out = lax.dot_general(MH[:, cols], high, ROWS_BY_ROWS, preferred_element_type=F32)
        out += lax.dot_general(ML[:, cols], high, ROWS_BY_ROWS, preferred_element_type=F32)
        return out + lax.dot_general(MH[:, cols], low, ROWS_BY_ROWS, preferred_element_type=F32)

    def chip_at(o):
        return ((y + o % 4) % 4) * 2 + (xl + o // 4) % 2

    def tile_products(t, cols):
        rows = pl.ds(pl.multiple_of(256 * chip_at(7 - t), 256), 256)
        return products(AH[rows, cols], AL[rows, cols], cols)

    loop(1, 8, lambda o: arrival(0, o).wait_recv())
    build_half(0)

    loop(1, 8, lambda o: arrival(1, o).wait_recv())

    halo = (
        copy(XA.at[1, 8, :, 128:256], XA.at[1, 0, :, 128:256], halo_s.at[0], halo_r.at[0], up, s),
        copy(XA.at[0, 1, :, 0:128], XA.at[0, 9, :, 0:128], halo_s.at[1], halo_r.at[1], down, s),
    )
    halo[0].start()
    halo[1].start()
    build_half(1)
    halo[0].wait()
    halo[1].wait()
    tail = XA[1, 0, :, 128:256]
    ghost = 2.0 * XA[0, 1, :, 0:1] - XA[0, 1, :, 1:2]
    XA[1, 0, :, 128:256] = jnp.where(a == 0, jnp.broadcast_to(ghost, (64, 128)), tail)
    head = XA[0, 9, :, 0:128]
    ghost = 2.0 * XA[1, 8, :, HALF - 1 : HALF] - XA[1, 8, :, HALF - 2 : HALF - 1]
    XA[0, 9, :, 0:128] = jnp.where(a == 15, jnp.broadcast_to(ghost, (64, 128)), head)
    lane = lax.broadcasted_iota(jnp.int32, (64, HALF), 1)

    def rates_of(q, b):
        x = XA[q, b + 1]
        before = XA[1 - q, b + q, :, HALF - 1 : HALF]
        after = XA[1 - q, b + 1 + q, :, 0:1]
        before = jnp.where(lane == 0, jnp.broadcast_to(before, x.shape), pltpu.roll(x, 1, 1))
        after = jnp.where(lane == HALF - 1, jnp.broadcast_to(after, x.shape), pltpu.roll(x, HALF - 1, 1))
        return 0.5 * (after - before)

    for q in range(2):
        def rate_rows(b):
            high, low = split(rates_of(q, b))
            LH[64:128, half_cols(8 * q + b)] = high
            LL[64:128, half_cols(8 * q + b)] = low

        loop(0, 8, rate_rows)
        rates_o[:, HALF * q : HALF * q + HALF] = rates_of(q, s)

    accl[...] = products(LH[...], LL[...], slice(0, SLAB))
    turn[0:272, :] = accl[...]
    turn[272:384, :] = jnp.zeros((112, 256), F32)
    for k in range(3):
        lines = turn[128 * k : 128 * k + 128, 0:128].T
        for t in range(16):
            lom[t % 2, t // 2, k] = lines[8 * t : 8 * t + 8, :]
        lines = turn[128 * k : 128 * k + 128, 128:256].T
        for t in range(8):
            lom[0, t, 3 + k] = lines[8 * t : 8 * t + 8, :]
            lom[1, t, 3 + k] = lines[8 * t : 8 * t + 8, :]

    def lo_pair():
        return copy(lom.at[1 - c], lomr, lc_s.at[8], lc_r.at[8], sibling, s)

    def lo_share(o):
        to = (chip + o) % 8
        return copy(lom.at[c, to], lor.at[o], lo_s.at[o], lo_r.at[o], to * 2 + c, s)

    def lo_times(o):
        part = LOT.at[chip]
        return copy(part, part, lt_s.at[o], lt_r.at[o], ((chip + o) % 8) * 2 + c, s)

    def lo_times_arrival(o):
        part = LOT.at[(chip + 8 - o) % 8]
        return copy(part, part, lt_s.at[o], lt_r.at[o], ((chip + o) % 8) * 2 + c, s)

    def lo_space(o):
        return copy(LOA.at[0, c], LOA.at[o, c], lx_s.at[o], lx_r.at[o], a, space_to(o))

    def lo_core(o):
        return copy(LOA.at[o, c], LOA.at[o, c], lc_s.at[o], lc_r.at[o], sibling, s)

    def lo_core_arrival(o):
        return copy(LOA.at[o, 1 - c], LOA.at[o, 1 - c], lc_s.at[o], lc_r.at[o], sibling, s)

    def lo_step_1():
        lo_pair().wait()
        lom[c] += lomr[...]
        loop(1, 8, lambda o: lo_share(o).start())

    def lo_step_2():
        loop(1, 8, lambda o: lo_share(o).wait_recv())
        lor[0] = lom[c, chip]
        los[...] = jnp.zeros((6, 8, 128), F32)

        def add(k):
            los[...] += lor[(chip + 8 - k) % 8]

        loop(0, 8, add)
        LOT[chip] = los[0:3]
        loop(1, 8, lambda o: lo_times(o).start())

    lane8 = lax.broadcasted_iota(jnp.int32, (8, 128), 1)

    def lo_step_3():
        loop(1, 8, lambda o: lo_times_arrival(o).wait_recv())
        packed = LOT[0, 2]
        for k in range(8):
            LOA[0, c, k] = LOT[k, 0]
            LOA[0, c, 8 + k] = LOT[k, 1]
            if k:
                packed = jnp.where(lane8 // 16 == k, pltpu.roll(LOT[k, 2], 16 * k, 1), packed)
        LOA[0, c, 16] = packed
        LOA[0, c, 17] = jnp.zeros((8, 128), F32)
        for k in range(3):
            LOA[0, c, 17, k : k + 1, :] = los[3 + k, 4:5, :]
        lo_core(0).start()
        loop(1, 8, lambda o: lo_space(o).start())

    def forward(o):
        lo_space(o).wait_recv()
        lo_core(o).start()

    lo_pair().start()

    def core_share(t):
        return copy(accs.at[t, 1 - c, 0:SENT], crecv.at[t], core_s.at[t], core_r.at[t], sibling, s)

    def y_share(o):
        to = ((y + o % 4) % 4) * 4 + xl * 2 + c
        return copy(accs.at[7 - o, c, 0:SENT], yrecv.at[o], y_s.at[o], y_r.at[o], to, s)

    def x_share():
        return copy(xsend, xrecv, x_s, x_r, y * 4 + (1 - xl) * 2 + c, s)

    def pass_on(t):
        core_share(t).wait_recv()
        accs[t, c, 0:SENT, :] += crecv[t]

        @pl.when(t % 4 < 3)
        def _():
            y_share(7 - t).start()

    def add_y(into, low):
        into[0:SENT] = accs[7 - low, c, 0:SENT, :]

        def add(o):
            y_share(o).wait_recv()
            into[0:SENT] += yrecv[o]

        loop(low + 1, low + 4, add)

    def tile(t):
        @pl.when(t == 7)
        def _():
            pass_on(6)

        out = tile_products(t, slice(0, SLAB))
        accs[t, 0] = out[:, 0:128]
        accs[t, 1] = out[:, 128:256]
        core_share(t).start()

        @pl.when((t > 0) & (t < 7))
        def _():
            pass_on(t - 1)

        @pl.when(t == 0)
        def _():
            lo_step_1()

        @pl.when(t == 2)
        def _():
            lo_step_2()

        @pl.when(t == 4)
        def _():
            lo_step_3()

        @pl.when(t == 6)
        def _():
            add_y(xsend, 4)
            x_share().start()

        @pl.when(t == 7)
        def _():
            loop(1, 8, forward)

    loop(0, 8, tile)
    pass_on(7)

    scale = 1.0 / (SLAB * TIMES)
    add_y(accl.at[:, 0:128], 0)
    x_share().wait_recv()
    turn[0:SENT, 0:128] = accl[0:SENT, 0:128] + xrecv[...]
    left, right, four = (turn[128 * k : 128 * k + 128, 0:128].T for k in range(3))

    def place(left, right, four):
        low = lax.broadcasted_iota(jnp.int32, left.shape, 1) < 2
        moved = pltpu.roll(right, 2, 1)
        return left, jnp.where(low, four, moved), jnp.where(low, moved, four)

    first, second, third = place(left, right, four)
    gram_o[0:128, 0:128] = first * scale
    gram_o[0:128, 128:256] = second * scale
    gram_o[0:128, 256:260] = third[:, 0:4] * scale
    parts = place(los[3], los[4], los[5])
    first, second, third = (jnp.where(c == 0, part[0:2, :], part[2:4, :]) * scale for part in parts)
    gram_o[128:130, 0:128] = first
    gram_o[128:130, 128:256] = second
    gram_o[128:130, 256:260] = third[:, 0:4]

    loop(0, 8, lambda o: lo_core_arrival(o).wait_recv())

    wide = lax.broadcasted_iota(jnp.int32, (136, 128), 1)
    carried = jnp.zeros((136, 128), F32)
    last = jnp.zeros((136, 128), F32)
    for b in range(8):
        o = ((xh + 2 - b // 4) % 2) * 4 + (z + 4 - b % 4) % 4
        ones = LOA[o, 0, 17]
        left = jnp.concatenate([LOA[o, t % 2, t // 2] for t in range(16)] + [ones], axis=0)
        right = jnp.concatenate([LOA[o, t % 2, 8 + t // 2] for t in range(16)] + [pltpu.roll(ones, 7, 0)], axis=0)
        packed = [LOA[o, t, 16] for t in range(2)]
        four = jnp.concatenate(
            [pltpu.roll(packed[t % 2], (128 - 16 * (t // 2)) % 128, 1) if t // 2 else packed[t % 2] for t in range(16)]
            + [pltpu.roll(ones, 6, 0)],
            axis=0,
        )
        shift = 4 * b
        first, second, third = (pltpu.roll(v, shift, 1) if b else v for v in place(left, right, four))
        GS[:, 256 * b : 256 * b + 128] = jnp.where(wide < shift, carried, first)
        GS[:, 256 * b + 128 : 256 * b + 256] = jnp.where(wide < shift, first, second)
        carried = jnp.where(wide < shift, second, third)
        modes = pltpu.roll(four, 25 + 8 * b, 1)
        last = jnp.where((wide >= 33 + 8 * b) & (wide < 41 + 8 * b), modes, last)
        if b == 7:
            last = jnp.where(wide == 32, pltpu.roll(four, 28, 1), last)
    GS[:, 2048:2176] = jnp.where(wide < 32, carried, last)
    side_o[0:1, :] = GS[128:129, 0:2145] * scale
    side_o[1:65, :] = GS[0:64, 0:2145] * scale
    rhs_o[...] = GS[64:128, 0:2145] * scale

    for q in range(2):
        loop(1, 8, lambda o: share(q, o).wait_send())
        loop(1, 8, lambda o: spread(q, o).wait_send())
    loop(1, 8, lambda o: lo_share(o).wait_send())
    loop(1, 8, lambda o: lo_times(o).wait_send())
    loop(1, 8, lambda o: lo_space(o).wait_send())
    loop(0, 8, lambda o: lo_core(o).wait_send())
    loop(0, 8, lambda t: core_share(t).wait_send())
    loop(1, 4, lambda o: y_share(o).wait_send())
    loop(5, 8, lambda o: y_share(o).wait_send())
    x_share().wait_send()


def hand_over_kernel(*refs):
    count = (len(refs) - 2) // 3
    given, final, held = refs[:count], refs[count : 2 * count], refs[2 * count : 3 * count]
    come, go = refs[-2:]
    arrive = [pltpu.make_async_copy(given[k], held[k], come.at[k]) for k in range(count)]
    leave = [pltpu.make_async_copy(held[k], final[k], go.at[k]) for k in range(count)]
    for each in arrive:
        each.start()
    for k in range(count):
        arrive[k].wait()
        leave[k].start()
    for each in leave:
        each.wait()


def hand_over(*arrays):
    anywhere = pl.BlockSpec(memory_space=pl.ANY)
    return pl.pallas_call(
        hand_over_kernel,
        out_shape=tuple(jax.ShapeDtypeStruct(each.shape, each.dtype) for each in arrays),
        in_specs=[anywhere] * len(arrays),
        out_specs=(anywhere,) * len(arrays),
        scratch_shapes=[pltpu.VMEM(each.shape, each.dtype) for each in arrays]
        + [pltpu.SemaphoreType.DMA((len(arrays),))] * 2,
        compiler_params=pltpu.CompilerParams(vmem_limit_bytes=60 << 20),
    )(*arrays)


def body(snapshots, basis):
    vmem = pl.BlockSpec(memory_space=pltpu.VMEM)
    dma = pltpu.SemaphoreType.DMA
    rates, gram_quad, gram_side, rhs = pl.pallas_call(
        kernel,
        out_shape=(
            jax.ShapeDtypeStruct((MODES, BLOCK), F32),
            jax.ShapeDtypeStruct((130, 260), F32),
            jax.ShapeDtypeStruct((65, 2145), F32),
            jax.ShapeDtypeStruct((64, 2145), F32),
        ),
        in_specs=[pl.BlockSpec(memory_space=pl.ANY), vmem],
        out_specs=(vmem, vmem, vmem, vmem),
        scratch_shapes=[
            pltpu.VMEM((2048, SLAB), BF16),
            pltpu.VMEM((2048, SLAB), BF16),
            pltpu.VMEM((MINE, SLAB), BF16),
            pltpu.VMEM((MINE, SLAB), BF16),
            pltpu.VMEM((256, SLAB), BF16),
            pltpu.VMEM((256, SLAB), BF16),
            pltpu.VMEM((2, 10, MODES, HALF), F32),
            pltpu.VMEM((8, 80, HALF), F32),
            pltpu.VMEM((64, HALF), F32),
            pltpu.VMEM((16, MODES, HALF), F32),
            pltpu.VMEM((16, MODES, HALF), F32),
            pltpu.VMEM((8, 2, MINE, 128), F32),
            pltpu.VMEM((8, SENT, 128), F32),
            pltpu.VMEM((8, SENT, 128), F32),
            pltpu.VMEM((SENT, 128), F32),
            pltpu.VMEM((SENT, 128), F32),
            pltpu.VMEM((MINE, 256), F32),
            pltpu.VMEM((384, 256), F32),
            pltpu.VMEM((2, 8, 6, 8, 128), F32),
            pltpu.VMEM((8, 6, 8, 128), F32),
            pltpu.VMEM((8, 6, 8, 128), F32),
            pltpu.VMEM((6, 8, 128), F32),
            pltpu.VMEM((8, 3, 8, 128), F32),
            pltpu.VMEM((8, 2, 18, 8, 128), F32),
            pltpu.VMEM((136, 2176), F32),
            dma((16,)), dma((16,)), dma((16,)), dma((16,)), dma((16,)), dma((2,)), dma((2,)),
            dma((8,)), dma((8,)), dma((8,)), dma((8,)), dma(()), dma(()),
            dma((8,)), dma((8,)), dma((8,)), dma((8,)), dma((8,)), dma((8,)), dma((9,)), dma((9,)),
        ],
        compiler_params=pltpu.CompilerParams(
            collective_id=0, has_side_effects=True, vmem_limit_bytes=60 << 20
        ),
    )(snapshots, basis.T)
    rates, gram_quad, gram_side, rhs = hand_over(rates, gram_quad, gram_side, rhs)
    return rates, gram_quad, gram_side, rhs.T


def solution(mesh):
    in_specs = (P("space", "tm"), P("space", None))
    out_specs = (P(None, ("tm", "space")), P("tm", "space"), P(), P())
    return jax.shard_map(body, mesh=mesh, in_specs=in_specs, out_specs=out_specs, check_vma=False)
```
